32 devices in a mesh: blk: 8 (over y, x, core), win: 4 (over z).
Axes of the slice: x: 2, y: 2, z: 4, core: 2. Of those that a mesh axis runs over, the one named last changes fastest.
Arguments:
- record: bfloat16 [4096, 4096], P('blk', 'win'), may hold values from -6 to 6
- deck_ids: int32 [32], replicated, may hold values from 0 to 1, as said below
- partners: int32 [32, 4], replicated, may hold values from 0 to 31, as said below
Outputs:
- correlations: bfloat16 [128, 64, 16384], P(('blk', 'win'))
The draws below stay inside these ranges and needn't reach their ends.
Inputs may be any that keep to these rules, and one draw needn't show every extreme that they name: `deck_ids`: 0 on the first deck and 1 on the second; non-decreasing in the block id (a single switch from 0 to 1), and both decks occur. Row b lists the partner blocks of block b. Take the blocks in groups of 4 consecutive ids: the partners of the blocks of one group are all different, and they name exactly 2 blocks of every group.
All inputs are finite; a program needn't handle non-finite values.
Results may differ from the reference program's by a relative error of at most 0.0075.
Values may be sent and summed in bfloat16 or wider, within the bound.
A program may use at most 128 MiB of HBM per device.

```python
import math
import jax
import jax.numpy as jnp
from jax import lax

BCH = 128
WS = 512
BINS = 128
LAGS = 64
PAIR_DEV = 4
WINDOWS = 8
SAMPLES = 4096
BLOCKS = 32
CHANNELS = 4096
PAIRS = 128
CAP = 2
N_BLK = 8
N_WIN = 4


def draw_deck_ids(key, part):
    deck_key = jax.random.fold_in(key, 7)
    boundary = jax.random.randint(deck_key, (), BLOCKS // 4, 3 * BLOCKS // 4 + 1)
    return (jnp.arange(BLOCKS, dtype=jnp.int32) >= boundary).astype(jnp.int32)


def draw_partners(key, part):
    pick_key = jax.random.fold_in(key, 11)
    order_key = jax.random.fold_in(key, 13)
    scores = jax.random.randint(pick_key, (N_BLK, N_BLK, N_WIN), 0, 1 << 20) * N_WIN + jnp.arange(N_WIN, dtype=jnp.int32)
    picked = jnp.argsort(scores, axis=-1)[:, :, :CAP]
    chosen_blocks = (jnp.arange(N_BLK, dtype=jnp.int32)[None, :, None] * N_WIN + picked).reshape(N_BLK, N_BLK * CAP)
    spread = N_BLK * CAP
    shuffle = jax.random.randint(order_key, (N_BLK, spread), 0, 1 << 20) * spread + jnp.arange(spread, dtype=jnp.int32)
    placing = jnp.argsort(shuffle, axis=-1)
    mixed = jnp.take_along_axis(chosen_blocks, placing, axis=-1)
    return mixed.reshape(BLOCKS, PAIR_DEV).astype(jnp.int32)


def block_scale(key, dims, split, smallest, top_value):
    level, own = 1.0, jax.random.fold_in(key, 6)
    for axis_at, shards_of in split:
        heights = jnp.exp(jax.random.uniform(jax.random.fold_in(own, axis_at), (shards_of,), jnp.float32, smallest / len(split), top_value / len(split)))
        level = level * jnp.repeat(heights, dims[axis_at] // shards_of).reshape([-1 if axis == axis_at else 1 for axis in range(len(dims))])
    return level


def scatter_about(rng, dims, deviation, reach, pieces=(), kind=jnp.bfloat16):
    loudness = block_scale(rng, dims, pieces, -0.22, 0.18) if pieces else 1.0
    array = jax.random.normal(rng, dims, jnp.float32) * deviation * loudness
    return jnp.minimum(jnp.maximum(array, -reach), reach).astype(kind)


def setup_inputs(seed: int = 0) -> dict:
    key_of = jax.random.split(jax.random.key(seed), 4)
    return {
        "record": scatter_about(key_of[0], (CHANNELS, SAMPLES), 1.0, 6.0, ((0, 8), (1, 4))),
        "deck_ids": draw_deck_ids(jax.random.fold_in(key_of[3], 71), 0),
        "partners": draw_partners(jax.random.fold_in(key_of[3], 71), 0),
    }


def forward_table():
    samples = jnp.arange(WS, dtype=jnp.int32)
    frequency = jnp.arange(1, BINS + 1, dtype=jnp.int32)
    phases = samples[:, None] * frequency[None, :] % WS
    angles = phases.astype(jnp.float32) * (2.0 * math.pi / WS)
    return jnp.concatenate([jnp.cos(angles), -jnp.sin(angles)], axis=1).astype(jnp.bfloat16)

def inverse_table():
    frequency = jnp.arange(1, BINS + 1, dtype=jnp.int32)
    shifts = jnp.arange(LAGS, dtype=jnp.int32) - LAGS // 2
    phases = frequency[:, None] * shifts[None, :] % WS
    angles = phases.astype(jnp.float32) * (2.0 * math.pi / WS)
    return jnp.stack([jnp.cos(angles), -jnp.sin(angles)], axis=0).astype(jnp.bfloat16)

def whiten(windowed, polarity):
    spectra = jnp.dot(windowed, forward_table(), preferred_element_type=jnp.float32)
    power_mean = lax.optimization_barrier(jnp.sum(spectra * spectra, axis=1)) / BINS
    factor = polarity / jnp.sqrt(power_mean + 1e-06)
    return (spectra * factor[:, None]).astype(jnp.bfloat16)

def correlate(own_block, partner, inverse):
    own_values = own_block.reshape(BCH, WINDOWS, 2, BINS).astype(jnp.float32)
    partner_values = partner.reshape(BCH, WINDOWS, 2, BINS).astype(jnp.float32)
    rotated = jnp.stack([own_values[:, :, 1], -own_values[:, :, 0]], axis=2)
    real_part = jnp.einsum('iwcf,jwcf->fij', own_values, partner_values)
    imag_part = jnp.einsum('iwcf,jwcf->fij', rotated, partner_values)
    cross_spec = jnp.stack([real_part, imag_part], axis=1).astype(jnp.bfloat16)
    lagged = jnp.einsum('fvij,vfl->lij', cross_spec.astype(jnp.float32), inverse.astype(jnp.float32))
    lag_scale = 1.0 / math.sqrt(WINDOWS * BINS)
    return (lagged * lag_scale).reshape(LAGS, BCH * BCH).astype(jnp.bfloat16)

def reference(record, deck_ids, partners):
    polarity = jnp.repeat(1.0 - 2.0 * deck_ids.astype(jnp.float32), BCH * WINDOWS)
    whitened = whiten(record.reshape(CHANNELS * WINDOWS, WS), polarity)
    blocks = whitened.reshape(BLOCKS, BCH, WINDOWS, 2 * BINS)
    inverse = inverse_table()
    flat_partners = partners.reshape(-1)

    def one_pair(pair_index):
        own_block = lax.dynamic_index_in_dim(blocks, pair_index // PAIR_DEV, 0, keepdims=False)
        partner = lax.dynamic_index_in_dim(blocks, flat_partners[pair_index], 0, keepdims=False)
        return correlate(own_block, partner, inverse)
    return lax.map(one_pair, jnp.arange(PAIRS, dtype=jnp.int32))
```

```python
import functools
import math

import jax
import jax.numpy as jnp
import numpy as np
from jax import lax
from jax.experimental import pallas as pl
from jax.experimental.pallas import tpu as pltpu
from jax.sharding import PartitionSpec as P

WS = 512
BINS = 128
LAGS = 64
PIECE_ROWS = 16
TILE = 8


def forward_table():
    phases = np.arange(WS)[:, None] * np.arange(1, BINS + 1)[None, :] % WS
    angles = phases * (2.0 * math.pi / WS)
    return jnp.asarray(np.concatenate([np.cos(angles), -np.sin(angles)], axis=1), jnp.bfloat16)


def lag_table(scale):
    shifts = np.arange(LAGS) - LAGS // 2
    phases = shifts[:, None] * np.arange(1, BINS + 1)[None, :] % WS
    angles = phases * (2.0 * math.pi / WS)
    table = np.stack([np.cos(angles), -np.sin(angles)], axis=0)
    return jnp.asarray(table, jnp.bfloat16).astype(jnp.float32) * scale


def whiten_kernel(block_rows, deck_ref, record_ref, table_ref, out_ref):
    pieces, blocks, rows, lanes = out_ref.shape
    windows = record_ref.shape[1] // WS
    lane_parts = windows * 2 * BINS // lanes
    for block in range(blocks):
        here = pl.ds(block * block_rows, block_rows)
        polarity = (1 - 2 * deck_ref[block]).astype(jnp.float32)
        values = []
        for window in range(windows):
            spectra = jnp.dot(
                record_ref[here, pl.ds(window * WS, WS)],
                table_ref[...],
                preferred_element_type=jnp.float32,
            )
            power = jnp.sum(spectra * spectra, axis=1, keepdims=True) / BINS
            values.append((spectra * (polarity / jnp.sqrt(power + 1e-06))).astype(jnp.bfloat16))
        whole = jnp.concatenate(values, axis=1)
        for piece in range(pieces):
            row, lane = piece // lane_parts, piece % lane_parts
            out_ref[piece, block] = whole[
                row * rows : (row + 1) * rows, lane * lanes : (lane + 1) * lanes
            ]


def whiten(record, decks, pieces, block_rows, rows, lanes):
    blocks = record.shape[0] // block_rows
    return pl.pallas_call(
        functools.partial(whiten_kernel, block_rows),
        out_shape=jax.ShapeDtypeStruct((pieces, blocks, rows, lanes), jnp.bfloat16),
        in_specs=[
            pl.BlockSpec(memory_space=pltpu.SMEM),
            pl.BlockSpec(memory_space=pltpu.VMEM),
            pl.BlockSpec(memory_space=pltpu.VMEM),
        ],
        out_specs=pl.BlockSpec(memory_space=pltpu.VMEM),
        compiler_params=pltpu.CompilerParams(vmem_limit_bytes=32 * 2**20),
    )(decks, record, forward_table())


def pick_kernel(ids_ref, full_ref, out_ref, sems):
    copies = []
    for item in range(out_ref.shape[0]):
        copies.append(
            pltpu.make_async_copy(full_ref.at[:, ids_ref[item]], out_ref.at[item], sems.at[item])
        )
        copies[-1].start()
    for copy in copies:
        copy.wait()


def pick(ids, full):
    slabs, _, rows, lanes = full.shape
    return pl.pallas_call(
        pick_kernel,
        out_shape=jax.ShapeDtypeStruct((ids.shape[0], slabs, rows, lanes), full.dtype),
        in_specs=[
            pl.BlockSpec(memory_space=pltpu.SMEM),
            pl.BlockSpec(memory_space=pl.ANY),
        ],
        out_specs=pl.BlockSpec(memory_space=pl.ANY),
        scratch_shapes=[pltpu.SemaphoreType.DMA((ids.shape[0],))],
    )(ids, full)


def correlate_kernel(lane_parts, items_ref, lags_ref, out_ref, own, partners, even, odd):
    pieces, blocks, slabs, rows, lanes = items_ref.shape
    step = pl.program_id(0)
    pairs = blocks - 1
    depth = own.shape[1]
    block_rows = own.shape[0]
    slab_lanes = lanes * lane_parts

    def shift(buffer, first):
        cosine, sine = lags_ref[0], lags_ref[1]
        for row in range(TILE):
            line = own[pl.ds(first + row, 1), :]
            for window in range(depth // (2 * BINS)):
                base = window * 2 * BINS
                real = line[:, base : base + BINS]
                imag = line[:, base + BINS : base + 2 * BINS]
                buffer[row * LAGS : (row + 1) * LAGS, base : base + BINS] = (
                    real * cosine + imag * sine
                ).astype(jnp.bfloat16)
                buffer[row * LAGS : (row + 1) * LAGS, base + BINS : base + 2 * BINS] = (
                    imag * cosine - real * sine
                ).astype(jnp.bfloat16)

    def multiply(buffer, first):
        total = jnp.dot(buffer[...], partners[...], preferred_element_type=jnp.float32)
        total = total.astype(jnp.bfloat16)
        for row in range(TILE):
            for pair in range(pairs):
                out_ref[pair, :, (first + row) * block_rows : (first + row + 1) * block_rows] = (
                    total[row * LAGS : (row + 1) * LAGS, pair * block_rows : (pair + 1) * block_rows]
                )

    @pl.when(step == 0)
    def _():
        for slab in range(slabs):
            for lane in range(lane_parts):
                at = slab * slab_lanes + lane * lanes
                parts = range(lane, pieces, lane_parts)
                mine = jnp.concatenate([items_ref[part, 0, slab] for part in parts], axis=0)
                own[:, at : at + lanes] = mine.astype(jnp.float32)
                for pair in range(pairs):
                    other = jnp.concatenate(
                        [items_ref[part, 1 + pair, slab] for part in parts], axis=0
                    )
                    partners[at : at + lanes, pair * block_rows : (pair + 1) * block_rows] = other.T
        shift(even, 0)

    first = step * 2 * TILE
    shift(odd, first + TILE)
    multiply(even, 0)
    shift(even, lax.rem(first + 2 * TILE, block_rows))
    multiply(odd, TILE)


def correlate(items, block_rows, lane_parts):
    pieces, blocks, slabs, rows, lanes = items.shape
    pairs = blocks - 1
    depth = slabs * lanes * lane_parts
    windows = depth // (2 * BINS)
    scale = 1.0 / math.sqrt(windows * BINS)
    return pl.pallas_call(
        functools.partial(correlate_kernel, lane_parts),
        grid=(block_rows // (2 * TILE),),
        out_shape=jax.ShapeDtypeStruct((pairs, LAGS, block_rows * block_rows), jnp.bfloat16),
        in_specs=[
            pl.BlockSpec(memory_space=pltpu.VMEM),
            pl.BlockSpec(memory_space=pltpu.VMEM),
        ],
        out_specs=pl.BlockSpec((pairs, LAGS, 2 * TILE * block_rows), lambda i: (0, 0, i)),
        scratch_shapes=[
            pltpu.VMEM((block_rows, depth), jnp.float32),
            pltpu.VMEM((depth, pairs * block_rows), jnp.bfloat16),
            pltpu.VMEM((TILE * LAGS, depth), jnp.bfloat16),
            pltpu.VMEM((TILE * LAGS, depth), jnp.bfloat16),
        ],
        compiler_params=pltpu.CompilerParams(vmem_limit_bytes=48 * 2**20),
        cost_estimate=pl.CostEstimate(
            flops=2 * LAGS * block_rows * depth * pairs * block_rows,
            bytes_accessed=pairs * LAGS * block_rows * block_rows * 2,
            transcendentals=0,
        ),
    )(items, lag_table(scale))


def shards(record, deck_ids, partners):
    groups = lax.axis_size("blk")
    members = lax.axis_size("win")
    group_index = lax.axis_index("blk")
    member_index = lax.axis_index("win")
    block_rows = record.shape[0] // members
    slab_lanes = record.shape[1] // WS * 2 * BINS
    row_parts = block_rows // PIECE_ROWS
    lane_parts = max(1, groups // row_parts)
    lanes = slab_lanes // lane_parts
    rows = block_rows * lane_parts // groups
    all_blocks = groups * members
    decks = lax.dynamic_slice_in_dim(deck_ids, group_index * members, members, 0)
    pieces = whiten(record, decks, groups, block_rows, rows, lanes)
    held = lax.all_to_all(pieces, "blk", split_axis=0, concat_axis=0, tiled=True)
    held = held.reshape(all_blocks, rows, lanes)
    full = lax.all_gather(held, "win", axis=0)
    own_ids = jnp.arange(groups, dtype=jnp.int32) * members + member_index
    rows_here = lax.dynamic_index_in_dim(
        partners.reshape(groups, members, -1), member_index, 1, keepdims=False
    )
    ids = jnp.concatenate([own_ids[:, None], rows_here], axis=1)
    chosen = pick(ids.reshape(-1), full)
    chosen = chosen.reshape(groups, ids.shape[1], members, rows, lanes)
    items = lax.all_to_all(chosen, "blk", split_axis=0, concat_axis=0, tiled=True)
    return correlate(items, block_rows, lane_parts)


def solution(mesh):
    return jax.shard_map(
        shards,
        mesh=mesh,
        in_specs=(P("blk", "win"), P(), P()),
        out_specs=P(("blk", "win"), None, None),
        check_vma=False,
    )
```

```python
import functools
import math

import jax
import jax.numpy as jnp
import numpy as np
from jax import lax
from jax.experimental import pallas as pl
from jax.experimental.pallas import tpu as pltpu
from jax.sharding import PartitionSpec as P

WS = 512
BINS = 128
LAGS = 64
PIECE_ROWS = 16
TILE = 8


def forward_table():
    phases = np.arange(WS)[:, None] * np.arange(1, BINS + 1)[None, :] % WS
    angles = phases * (2.0 * math.pi / WS)
    return jnp.asarray(np.concatenate([np.cos(angles), -np.sin(angles)], axis=1), jnp.bfloat16)


def lag_table(scale):
    shifts = np.arange(LAGS) - LAGS // 2
    phases = shifts[:, None] * np.arange(1, BINS + 1)[None, :] % WS
    angles = phases * (2.0 * math.pi / WS)
    table = np.stack([np.cos(angles), -np.sin(angles)], axis=0)
    return jnp.asarray(table, jnp.bfloat16).astype(jnp.float32) * scale


def whiten_kernel(block_rows, deck_ref, record_ref, table_ref, out_ref):
    pieces, blocks, rows, lanes = out_ref.shape
    windows = record_ref.shape[1] // WS
    lane_parts = windows * 2 * BINS // lanes
    for block in range(blocks):
        here = pl.ds(block * block_rows, block_rows)
        polarity = (1 - 2 * deck_ref[block]).astype(jnp.float32)
        values = []
        for window in range(windows):
            spectra = jnp.dot(
                record_ref[here, pl.ds(window * WS, WS)],
                table_ref[...],
                preferred_element_type=jnp.float32,
            )
            power = jnp.sum(spectra * spectra, axis=1, keepdims=True) / BINS
            values.append((spectra * (polarity / jnp.sqrt(power + 1e-06))).astype(jnp.bfloat16))
        whole = jnp.concatenate(values, axis=1)
        for piece in range(pieces):
            row, lane = piece // lane_parts, piece % lane_parts
            out_ref[piece, block] = whole[
                row * rows : (row + 1) * rows, lane * lanes : (lane + 1) * lanes
            ]


def whiten(record, decks, pieces, block_rows, rows, lanes):
    blocks = record.shape[0] // block_rows
    return pl.pallas_call(
        functools.partial(whiten_kernel, block_rows),
        out_shape=jax.ShapeDtypeStruct((pieces, blocks, rows, lanes), jnp.bfloat16),
        in_specs=[
            pl.BlockSpec(memory_space=pltpu.SMEM),
            pl.BlockSpec(memory_space=pltpu.VMEM),
            pl.BlockSpec(memory_space=pltpu.VMEM),
        ],
        out_specs=pl.BlockSpec(memory_space=pltpu.VMEM),
        compiler_params=pltpu.CompilerParams(vmem_limit_bytes=32 * 2**20),
    )(decks, record, forward_table())


def pick_kernel(ids_ref, full_ref, out_ref):
    def one_item(item, carry):
        out_ref[item] = full_ref[:, ids_ref[item]]
        return carry

    lax.fori_loop(0, out_ref.shape[0], one_item, 0)


def pick(ids, full):
    slabs, _, rows, lanes = full.shape
    return pl.pallas_call(
        pick_kernel,
        out_shape=jax.ShapeDtypeStruct((ids.shape[0], slabs, rows, lanes), full.dtype),
        in_specs=[
            pl.BlockSpec(memory_space=pltpu.SMEM),
            pl.BlockSpec(memory_space=pltpu.VMEM),
        ],
        out_specs=pl.BlockSpec(memory_space=pltpu.VMEM),
        compiler_params=pltpu.CompilerParams(vmem_limit_bytes=32 * 2**20),
    )(ids, full)


def correlate_kernel(lane_parts, items_ref, lags_ref, out_ref, own, partners, even, odd):
    pieces, blocks, slabs, rows, lanes = items_ref.shape
    step = pl.program_id(0)
    pairs = blocks - 1
    depth = own.shape[1]
    block_rows = own.shape[0]
    slab_lanes = lanes * lane_parts

    def shift(buffer, first):
        cosine, sine = lags_ref[0], lags_ref[1]
        for row in range(TILE):
            line = own[pl.ds(first + row, 1), :]
            for window in range(depth // (2 * BINS)):
                base = window * 2 * BINS
                real = line[:, base : base + BINS]
                imag = line[:, base + BINS : base + 2 * BINS]
                buffer[row * LAGS : (row + 1) * LAGS, base : base + BINS] = (
                    real * cosine + imag * sine
                ).astype(jnp.bfloat16)
                buffer[row * LAGS : (row + 1) * LAGS, base + BINS : base + 2 * BINS] = (
                    imag * cosine - real * sine
                ).astype(jnp.bfloat16)

    def multiply(buffer, first):
        total = jnp.dot(buffer[...], partners[...], preferred_element_type=jnp.float32)
        total = total.astype(jnp.bfloat16)
        for row in range(TILE):
            for pair in range(pairs):
                out_ref[pair, :, (first + row) * block_rows : (first + row + 1) * block_rows] = (
                    total[row * LAGS : (row + 1) * LAGS, pair * block_rows : (pair + 1) * block_rows]
                )

    @pl.when(step == 0)
    def _():
        for slab in range(slabs):
            for lane in range(lane_parts):
                at = slab * slab_lanes + lane * lanes
                parts = range(lane, pieces, lane_parts)
                mine = jnp.concatenate([items_ref[part, 0, slab] for part in parts], axis=0)
                own[:, at : at + lanes] = mine.astype(jnp.float32)
                for pair in range(pairs):
                    other = jnp.concatenate(
                        [items_ref[part, 1 + pair, slab] for part in parts], axis=0
                    )
                    partners[at : at + lanes, pair * block_rows : (pair + 1) * block_rows] = other.T
        shift(even, 0)

    first = step * 2 * TILE
    shift(odd, first + TILE)
    multiply(even, 0)
    shift(even, lax.rem(first + 2 * TILE, block_rows))
    multiply(odd, TILE)


def correlate(items, block_rows, lane_parts):
    pieces, blocks, slabs, rows, lanes = items.shape
    pairs = blocks - 1
    depth = slabs * lanes * lane_parts
    windows = depth // (2 * BINS)
    scale = 1.0 / math.sqrt(windows * BINS)
    return pl.pallas_call(
        functools.partial(correlate_kernel, lane_parts),
        grid=(block_rows // (2 * TILE),),
        out_shape=jax.ShapeDtypeStruct((pairs, LAGS, block_rows * block_rows), jnp.bfloat16),
        in_specs=[
            pl.BlockSpec(memory_space=pltpu.VMEM),
            pl.BlockSpec(memory_space=pltpu.VMEM),
        ],
        out_specs=pl.BlockSpec((pairs, LAGS, 2 * TILE * block_rows), lambda i: (0, 0, i)),
        scratch_shapes=[
            pltpu.VMEM((block_rows, depth), jnp.float32),
            pltpu.VMEM((depth, pairs * block_rows), jnp.bfloat16),
            pltpu.VMEM((TILE * LAGS, depth), jnp.bfloat16),
            pltpu.VMEM((TILE * LAGS, depth), jnp.bfloat16),
        ],
        compiler_params=pltpu.CompilerParams(vmem_limit_bytes=48 * 2**20),
        cost_estimate=pl.CostEstimate(
            flops=2 * LAGS * block_rows * depth * pairs * block_rows,
            bytes_accessed=pairs * LAGS * block_rows * block_rows * 2,
            transcendentals=0,
        ),
    )(items, lag_table(scale))


def shards(record, deck_ids, partners):
    groups = lax.axis_size("blk")
    members = lax.axis_size("win")
    group_index = lax.axis_index("blk")
    member_index = lax.axis_index("win")
    block_rows = record.shape[0] // members
    slab_lanes = record.shape[1] // WS * 2 * BINS
    row_parts = block_rows // PIECE_ROWS
    lane_parts = max(1, groups // row_parts)
    lanes = slab_lanes // lane_parts
    rows = block_rows * lane_parts // groups
    all_blocks = groups * members
    decks = lax.dynamic_slice_in_dim(deck_ids, group_index * members, members, 0)
    pieces = whiten(record, decks, groups, block_rows, rows, lanes)
    held = lax.all_to_all(pieces, "blk", split_axis=0, concat_axis=0, tiled=True)
    held = held.reshape(all_blocks, rows, lanes)
    full = lax.all_gather(held, "win", axis=0)
    own_ids = jnp.arange(groups, dtype=jnp.int32) * members + member_index
    rows_here = lax.dynamic_index_in_dim(
        partners.reshape(groups, members, -1), member_index, 1, keepdims=False
    )
    ids = jnp.concatenate([own_ids[:, None], rows_here], axis=1)
    chosen = pick(ids.reshape(-1), full)
    chosen = chosen.reshape(groups, ids.shape[1], members, rows, lanes)
    items = lax.all_to_all(chosen, "blk", split_axis=0, concat_axis=0, tiled=True)
    return correlate(items, block_rows, lane_parts)


def solution(mesh):
    return jax.shard_map(
        shards,
        mesh=mesh,
        in_specs=(P("blk", "win"), P(), P()),
        out_specs=P(("blk", "win"), None, None),
        check_vma=False,
    )
```

```python
import functools
import math

import jax
import jax.numpy as jnp
import numpy as np
from jax import lax
from jax.experimental import pallas as pl
from jax.experimental.pallas import tpu as pltpu
from jax.sharding import PartitionSpec as P

WS = 512
BINS = 128
LAGS = 64
PIECE_ROWS = 16
LANES = 128
TILE = 8


def forward_table():
    phases = np.arange(WS)[:, None] * np.arange(1, BINS + 1)[None, :] % WS
    angles = phases * (2.0 * math.pi / WS)
    return jnp.asarray(np.concatenate([np.cos(angles), -np.sin(angles)], axis=1), jnp.bfloat16)


def lag_table(scale):
    shifts = np.arange(LAGS) - LAGS // 2
    phases = shifts[:, None] * np.arange(1, BINS + 1)[None, :] % WS
    angles = phases * (2.0 * math.pi / WS)
    table = np.stack([np.cos(angles), -np.sin(angles)], axis=0)
    return jnp.asarray(table, jnp.bfloat16).astype(jnp.float32) * scale


def whiten_kernel(block_rows, deck_ref, record_ref, table_ref, out_ref):
    chunks, pieces, blocks, rows, chunk_lanes = out_ref.shape
    windows = record_ref.shape[1] // WS
    lane_parts = windows * 2 * BINS // (chunks * chunk_lanes)
    for block in range(blocks):
        here = pl.ds(block * block_rows, block_rows)
        polarity = (1 - 2 * deck_ref[block]).astype(jnp.float32)
        values = []
        for window in range(windows):
            spectra = jnp.dot(
                record_ref[here, pl.ds(window * WS, WS)],
                table_ref[...],
                preferred_element_type=jnp.float32,
            )
            power = jnp.sum(spectra * spectra, axis=1, keepdims=True) / BINS
            values.append((spectra * (polarity / jnp.sqrt(power + 1e-06))).astype(jnp.bfloat16))
        whole = jnp.concatenate(values, axis=1)
        for piece in range(pieces):
            row, lane = piece // lane_parts, piece % lane_parts
            for chunk in range(chunks):
                at = (lane * chunks + chunk) * chunk_lanes
                out_ref[chunk, piece, block] = whole[
                    row * rows : (row + 1) * rows, at : at + chunk_lanes
                ]


def whiten(record, decks, block_rows, shape):
    return pl.pallas_call(
        functools.partial(whiten_kernel, block_rows),
        out_shape=jax.ShapeDtypeStruct(shape, jnp.bfloat16),
        in_specs=[
            pl.BlockSpec(memory_space=pltpu.SMEM),
            pl.BlockSpec(memory_space=pltpu.VMEM),
            pl.BlockSpec(memory_space=pltpu.VMEM),
        ],
        out_specs=pl.BlockSpec(memory_space=pltpu.VMEM),
        compiler_params=pltpu.CompilerParams(vmem_limit_bytes=32 * 2**20),
    )(decks, record, forward_table())


def exchange_kernel(
    groups, members, ids_ref, pieces_ref, items_ref, chosen, spread_send, spread_recv,
    up_send, up_recv, down_send, down_recv, give_send, give_recv, local, *full
):
    chunks, _, blocks = pieces_ref.shape[:3]
    wanted = items_ref.shape[2]
    group = lax.axis_index("blk")
    member = lax.axis_index("win")
    mesh_id = pl.DeviceIdType.MESH

    barrier = pltpu.get_barrier_semaphore()
    for offset in range(1, groups):
        pl.semaphore_signal(
            barrier, inc=1, device_id=(lax.rem(group + offset, groups), member),
            device_id_type=mesh_id,
        )

    @pl.when(member > 0)
    def _():
        pl.semaphore_signal(
            barrier, inc=1, device_id=(group, member - 1), device_id_type=mesh_id
        )

    @pl.when(member < members - 1)
    def _():
        pl.semaphore_signal(
            barrier, inc=1, device_id=(group, member + 1), device_id_type=mesh_id
        )

    beside = jnp.where(member > 0, 1, 0) + jnp.where(member < members - 1, 1, 0)
    pl.semaphore_wait(barrier, groups - 1 + beside)

    def spread(chunk, offset):
        peer = lax.rem(group + offset, groups)
        return pltpu.make_async_remote_copy(
            src_ref=pieces_ref.at[chunk, peer],
            dst_ref=full[chunk].at[member, pl.ds(group * blocks, blocks)],
            send_sem=spread_send.at[chunk, offset],
            recv_sem=spread_recv.at[chunk, offset],
            device_id=(peer, member),
            device_id_type=mesh_id,
        )

    def arrived(chunk, offset):
        peer = lax.rem(group + groups - offset, groups)
        here = full[chunk].at[member, pl.ds(peer * blocks, blocks)]
        return pltpu.make_async_remote_copy(
            src_ref=here,
            dst_ref=here,
            send_sem=spread_send.at[chunk, offset],
            recv_sem=spread_recv.at[chunk, offset],
            device_id=(peer, member),
            device_id_type=mesh_id,
        )

    def kept(chunk):
        return pltpu.make_async_copy(
            pieces_ref.at[chunk, group],
            full[chunk].at[member, pl.ds(group * blocks, blocks)],
            local.at[0, chunk],
        )

    def up(chunk, step, slab):
        return pltpu.make_async_remote_copy(
            src_ref=full[chunk].at[slab],
            dst_ref=full[chunk].at[slab],
            send_sem=up_send.at[chunk, step],
            recv_sem=up_recv.at[chunk, step],
            device_id=(group, member + 1),
            device_id_type=mesh_id,
        )

    def down(chunk, step, slab):
        return pltpu.make_async_remote_copy(
            src_ref=full[chunk].at[slab],
            dst_ref=full[chunk].at[slab],
            send_sem=down_send.at[chunk, step],
            recv_sem=down_recv.at[chunk, step],
            device_id=(group, member - 1),
            device_id_type=mesh_id,
        )

    def forward(chunk, step, act):
        @pl.when((member < members - 1) & (member >= step))
        def _():
            act(up(chunk, step, member - step))

        @pl.when((member > 0) & (member + step <= members - 1))
        def _():
            act(down(chunk, step, member + step))

    def receive(chunk, step):
        @pl.when(member >= step + 1)
        def _():
            up(chunk, step, member - 1 - step).wait_recv()

        @pl.when(member + 1 + step <= members - 1)
        def _():
            down(chunk, step, member + 1 + step).wait_recv()

    def open_chunk(chunk):
        kept(chunk).wait()
        for offset in range(1, groups):
            arrived(chunk, offset).wait_recv()
        forward(chunk, 0, lambda copy: copy.start())

    def give(chunk, offset):
        peer = lax.rem(group + offset, groups)
        return pltpu.make_async_remote_copy(
            src_ref=chosen.at[chunk, offset],
            dst_ref=items_ref.at[chunk, group],
            send_sem=give_send.at[chunk, offset],
            recv_sem=give_recv.at[chunk, offset],
            device_id=(peer, member),
            device_id_type=mesh_id,
        )

    def given(chunk, offset):
        peer = lax.rem(group + groups - offset, groups)
        return pltpu.make_async_remote_copy(
            src_ref=chosen.at[chunk, offset],
            dst_ref=items_ref.at[chunk, peer],
            send_sem=give_send.at[chunk, offset],
            recv_sem=give_recv.at[chunk, offset],
            device_id=(peer, member),
            device_id_type=mesh_id,
        )

    def mine(chunk):
        return pltpu.make_async_copy(
            chosen.at[chunk, 0], items_ref.at[chunk, group], local.at[1, chunk]
        )

    for chunk in range(chunks):
        for offset in range(1, groups):
            spread(chunk, offset).start()
        kept(chunk).start()
    open_chunk(0)
    for chunk in range(chunks):
        for step in range(1, members - 1):
            receive(chunk, step - 1)
            forward(chunk, step, lambda copy: copy.start())
        if chunk + 1 < chunks:
            open_chunk(chunk + 1)
        receive(chunk, members - 2)
        for offset in list(range(1, groups)) + [0]:
            peer = lax.rem(group + offset, groups)
            for slot in range(wanted):
                chosen[chunk, offset, slot] = full[chunk][:, ids_ref[peer * wanted + slot]]
            if offset:
                give(chunk, offset).start()
            else:
                mine(chunk).start()
    for chunk in range(chunks):
        for step in range(members - 1):
            forward(chunk, step, lambda copy: copy.wait_send())
        for offset in range(1, groups):
            spread(chunk, offset).wait_send()
            give(chunk, offset).wait_send()
            given(chunk, offset).wait_recv()
        mine(chunk).wait()


def exchange(ids, pieces, groups, members):
    chunks, _, blocks, rows, lanes = pieces.shape
    wanted = ids.shape[0] // groups
    dma = pltpu.SemaphoreType.DMA
    return pl.pallas_call(
        functools.partial(exchange_kernel, groups, members),
        out_shape=jax.ShapeDtypeStruct(
            (chunks, groups, wanted, members, rows, lanes), pieces.dtype
        ),
        in_specs=[
            pl.BlockSpec(memory_space=pltpu.SMEM),
            pl.BlockSpec(memory_space=pl.ANY),
        ],
        out_specs=pl.BlockSpec(memory_space=pl.ANY),
        scratch_shapes=[
            pltpu.VMEM((chunks, groups, wanted, members, rows, lanes), pieces.dtype),
            dma((chunks, groups)),
            dma((chunks, groups)),
            dma((chunks, members)),
            dma((chunks, members)),
            dma((chunks, members)),
            dma((chunks, members)),
            dma((chunks, groups)),
            dma((chunks, groups)),
            dma((2, chunks)),
        ]
        + [
            pltpu.VMEM((members, groups * blocks, rows, lanes), pieces.dtype)
            for _ in range(chunks)
        ],
        compiler_params=pltpu.CompilerParams(
            collective_id=0, has_side_effects=True, vmem_limit_bytes=32 * 2**20
        ),
    )(ids, pieces)


def correlate_kernel(lane_parts, items_ref, lags_ref, out_ref, own, partners, even, odd):
    chunks, pieces, blocks, slabs, rows, chunk_lanes = items_ref.shape
    step = pl.program_id(0)
    pairs = blocks - 1
    depth = own.shape[1]
    block_rows = own.shape[0]
    parts_of_slab = lane_parts * chunks

    def shift(buffer, first):
        cosine, sine = lags_ref[0], lags_ref[1]
        for row in range(TILE):
            line = own[pl.ds(first + row, 1), :]
            for window in range(depth // (2 * BINS)):
                base = window * 2 * BINS
                real = line[:, base : base + BINS]
                imag = line[:, base + BINS : base + 2 * BINS]
                buffer[row * LAGS : (row + 1) * LAGS, base : base + BINS] = (
                    real * cosine + imag * sine
                ).astype(jnp.bfloat16)
                buffer[row * LAGS : (row + 1) * LAGS, base + BINS : base + 2 * BINS] = (
                    imag * cosine - real * sine
                ).astype(jnp.bfloat16)

    def multiply(buffer, first):
        total = jnp.dot(buffer[...], partners[...], preferred_element_type=jnp.float32)
        total = total.astype(jnp.bfloat16)
        for row in range(TILE):
            for pair in range(pairs):
                out_ref[pair, :, (first + row) * block_rows : (first + row + 1) * block_rows] = (
                    total[row * LAGS : (row + 1) * LAGS, pair * block_rows : (pair + 1) * block_rows]
                )

    @pl.when(step == 0)
    def _():
        for slab in range(slabs):
            for place in range(parts_of_slab):
                lane, chunk = place // chunks, place % chunks
                at = (slab * parts_of_slab + place) * chunk_lanes
                parts = range(lane, pieces, lane_parts)
                mine = jnp.concatenate([items_ref[chunk, part, 0, slab] for part in parts], axis=0)
                own[:, at : at + chunk_lanes] = mine.astype(jnp.float32)
                for pair in range(pairs):
                    other = jnp.concatenate(
                        [items_ref[chunk, part, 1 + pair, slab] for part in parts], axis=0
                    )
                    columns = slice(pair * block_rows, (pair + 1) * block_rows)
                    partners[at : at + chunk_lanes, columns] = other.T
        shift(even, 0)

    first = step * 2 * TILE
    shift(odd, first + TILE)
    multiply(even, 0)
    shift(even, lax.rem(first + 2 * TILE, block_rows))
    multiply(odd, TILE)


def correlate(items, block_rows, lane_parts):
    chunks, _, blocks, slabs, _, chunk_lanes = items.shape
    pairs = blocks - 1
    depth = slabs * chunks * chunk_lanes * lane_parts
    windows = depth // (2 * BINS)
    scale = 1.0 / math.sqrt(windows * BINS)
    return pl.pallas_call(
        functools.partial(correlate_kernel, lane_parts),
        grid=(block_rows // (2 * TILE),),
        out_shape=jax.ShapeDtypeStruct((pairs, LAGS, block_rows * block_rows), jnp.bfloat16),
        in_specs=[
            pl.BlockSpec(memory_space=pltpu.VMEM),
            pl.BlockSpec(memory_space=pltpu.VMEM),
        ],
        out_specs=pl.BlockSpec((pairs, LAGS, 2 * TILE * block_rows), lambda i: (0, 0, i)),
        scratch_shapes=[
            pltpu.VMEM((block_rows, depth), jnp.float32),
            pltpu.VMEM((depth, pairs * block_rows), jnp.bfloat16),
            pltpu.VMEM((TILE * LAGS, depth), jnp.bfloat16),
            pltpu.VMEM((TILE * LAGS, depth), jnp.bfloat16),
        ],
        compiler_params=pltpu.CompilerParams(vmem_limit_bytes=48 * 2**20),
        cost_estimate=pl.CostEstimate(
            flops=2 * LAGS * block_rows * depth * pairs * block_rows,
            bytes_accessed=pairs * LAGS * block_rows * block_rows * 2,
            transcendentals=0,
        ),
    )(items, lag_table(scale))


def shards(record, deck_ids, partners):
    groups = lax.axis_size("blk")
    members = lax.axis_size("win")
    group_index = lax.axis_index("blk")
    member_index = lax.axis_index("win")
    block_rows = record.shape[0] // members
    slab_lanes = record.shape[1] // WS * 2 * BINS
    row_parts = block_rows // PIECE_ROWS
    lane_parts = max(1, groups // row_parts)
    lanes = slab_lanes // lane_parts
    rows = block_rows * lane_parts // groups
    chunks = lanes // LANES
    decks = lax.dynamic_slice_in_dim(deck_ids, group_index * members, members, 0)
    pieces = whiten(record, decks, block_rows, (chunks, groups, members, rows, LANES))
    own_ids = jnp.arange(groups, dtype=jnp.int32) * members + member_index
    rows_here = lax.dynamic_index_in_dim(
        partners.reshape(groups, members, -1), member_index, 1, keepdims=False
    )
    ids = jnp.concatenate([own_ids[:, None], rows_here], axis=1)
    items = exchange(ids.reshape(-1), pieces, groups, members)
    return correlate(items, block_rows, lane_parts)


def solution(mesh):
    return jax.shard_map(
        shards,
        mesh=mesh,
        in_specs=(P("blk", "win"), P(), P()),
        out_specs=P(("blk", "win"), None, None),
        check_vma=False,
    )
```

```python
import functools
import math

import jax
import jax.numpy as jnp
import numpy as np
from jax import lax
from jax.experimental import pallas as pl
from jax.experimental.pallas import tpu as pltpu
from jax.sharding import PartitionSpec as P

WS = 512
BINS = 128
LAGS = 64
PIECE_ROWS = 16
LANES = 128
TILE = 8


def forward_table():
    phases = np.arange(WS)[:, None] * np.arange(1, BINS + 1)[None, :] % WS
    angles = phases * (2.0 * math.pi / WS)
    return jnp.asarray(np.concatenate([np.cos(angles), -np.sin(angles)], axis=1), jnp.bfloat16)


def lag_table(scale):
    shifts = np.arange(LAGS) - LAGS // 2
    phases = shifts[:, None] * np.arange(1, BINS + 1)[None, :] % WS
    angles = phases * (2.0 * math.pi / WS)
    table = np.stack([np.cos(angles), -np.sin(angles)], axis=0)
    return jnp.asarray(table, jnp.bfloat16).astype(jnp.float32) * scale


def whiten_kernel(block_rows, deck_ref, record_ref, table_ref, out_ref):
    chunks, pieces, blocks, rows, chunk_lanes = out_ref.shape
    windows = record_ref.shape[1] // WS
    lane_parts = windows * 2 * BINS // (chunks * chunk_lanes)
    for block in range(blocks):
        here = pl.ds(block * block_rows, block_rows)
        polarity = (1 - 2 * deck_ref[block]).astype(jnp.float32)
        values = []
        for window in range(windows):
            spectra = jnp.dot(
                record_ref[here, pl.ds(window * WS, WS)],
                table_ref[...],
                preferred_element_type=jnp.float32,
            )
            power = jnp.sum(spectra * spectra, axis=1, keepdims=True) / BINS
            values.append((spectra * (polarity / jnp.sqrt(power + 1e-06))).astype(jnp.bfloat16))
        whole = jnp.concatenate(values, axis=1)
        for piece in range(pieces):
            row, lane = piece // lane_parts, piece % lane_parts
            for chunk in range(chunks):
                at = (lane * chunks + chunk) * chunk_lanes
                out_ref[chunk, piece, block] = whole[
                    row * rows : (row + 1) * rows, at : at + chunk_lanes
                ]


def whiten(record, decks, block_rows, shape):
    return pl.pallas_call(
        functools.partial(whiten_kernel, block_rows),
        out_shape=jax.ShapeDtypeStruct(shape, jnp.bfloat16),
        in_specs=[
            pl.BlockSpec(memory_space=pltpu.SMEM),
            pl.BlockSpec(memory_space=pltpu.VMEM),
            pl.BlockSpec(memory_space=pltpu.VMEM),
        ],
        out_specs=pl.BlockSpec(memory_space=pltpu.VMEM),
        compiler_params=pltpu.CompilerParams(vmem_limit_bytes=32 * 2**20),
    )(decks, record, forward_table())


def exchange_kernel(
    groups, members, ids_ref, pieces_ref, items_ref, chosen, spread_send, spread_recv,
    up_send, up_recv, down_send, down_recv, give_send, give_recv, local, *full
):
    chunks, _, blocks = pieces_ref.shape[:3]
    wanted = items_ref.shape[2]
    group = lax.axis_index("blk")
    member = lax.axis_index("win")
    mesh_id = pl.DeviceIdType.MESH

    barrier = pltpu.get_barrier_semaphore()
    for offset in range(1, groups):
        pl.semaphore_signal(
            barrier, inc=1, device_id=(lax.rem(group + offset, groups), member),
            device_id_type=mesh_id,
        )

    @pl.when(member > 0)
    def _():
        pl.semaphore_signal(
            barrier, inc=1, device_id=(group, member - 1), device_id_type=mesh_id
        )

    @pl.when(member < members - 1)
    def _():
        pl.semaphore_signal(
            barrier, inc=1, device_id=(group, member + 1), device_id_type=mesh_id
        )

    beside = jnp.where(member > 0, 1, 0) + jnp.where(member < members - 1, 1, 0)
    pl.semaphore_wait(barrier, groups - 1 + beside)

    def spread(chunk, offset):
        peer = lax.rem(group + offset, groups)
        return pltpu.make_async_remote_copy(
            src_ref=pieces_ref.at[chunk, peer],
            dst_ref=full[chunk].at[member, pl.ds(group * blocks, blocks)],
            send_sem=spread_send.at[chunk, offset],
            recv_sem=spread_recv.at[chunk, offset],
            device_id=(peer, member),
            device_id_type=mesh_id,
        )

    def arrived(chunk, offset):
        peer = lax.rem(group + groups - offset, groups)
        here = full[chunk].at[member, pl.ds(peer * blocks, blocks)]
        return pltpu.make_async_remote_copy(
            src_ref=here,
            dst_ref=here,
            send_sem=spread_send.at[chunk, offset],
            recv_sem=spread_recv.at[chunk, offset],
            device_id=(peer, member),
            device_id_type=mesh_id,
        )

    def kept(chunk):
        return pltpu.make_async_copy(
            pieces_ref.at[chunk, group],
            full[chunk].at[member, pl.ds(group * blocks, blocks)],
            local.at[0, chunk],
        )

    def up(chunk, step, slab):
        return pltpu.make_async_remote_copy(
            src_ref=full[chunk].at[slab],
            dst_ref=full[chunk].at[slab],
            send_sem=up_send.at[chunk, step],
            recv_sem=up_recv.at[chunk, step],
            device_id=(group, member + 1),
            device_id_type=mesh_id,
        )

    def down(chunk, step, slab):
        return pltpu.make_async_remote_copy(
            src_ref=full[chunk].at[slab],
            dst_ref=full[chunk].at[slab],
            send_sem=down_send.at[chunk, step],
            recv_sem=down_recv.at[chunk, step],
            device_id=(group, member - 1),
            device_id_type=mesh_id,
        )

    def forward(chunk, step, act):
        @pl.when((member < members - 1) & (member >= step))
        def _():
            act(up(chunk, step, member - step))

        @pl.when((member > 0) & (member + step <= members - 1))
        def _():
            act(down(chunk, step, member + step))

    def receive(chunk, step):
        @pl.when(member >= step + 1)
        def _():
            up(chunk, step, member - 1 - step).wait_recv()

        @pl.when(member + 1 + step <= members - 1)
        def _():
            down(chunk, step, member + 1 + step).wait_recv()

    def open_chunk(chunk):
        kept(chunk).wait()
        for offset in range(1, groups):
            arrived(chunk, offset).wait_recv()
        forward(chunk, 0, lambda copy: copy.start())

    def give(chunk, offset):
        peer = lax.rem(group + offset, groups)
        return pltpu.make_async_remote_copy(
            src_ref=chosen.at[chunk, offset],
            dst_ref=items_ref.at[chunk, group],
            send_sem=give_send.at[chunk, offset],
            recv_sem=give_recv.at[chunk, offset],
            device_id=(peer, member),
            device_id_type=mesh_id,
        )

    def given(chunk, offset):
        peer = lax.rem(group + groups - offset, groups)
        return pltpu.make_async_remote_copy(
            src_ref=chosen.at[chunk, offset],
            dst_ref=items_ref.at[chunk, peer],
            send_sem=give_send.at[chunk, offset],
            recv_sem=give_recv.at[chunk, offset],
            device_id=(peer, member),
            device_id_type=mesh_id,
        )

    def mine(chunk):
        return pltpu.make_async_copy(
            chosen.at[chunk, 0], items_ref.at[chunk, group], local.at[1, chunk]
        )

    for chunk in range(chunks):
        for offset in range(1, groups):
            spread(chunk, offset).start()
        kept(chunk).start()
    open_chunk(0)
    for chunk in range(chunks):
        if chunk + 1 < chunks:
            open_chunk(chunk + 1)
        for step in range(1, members - 1):
            receive(chunk, step - 1)
            forward(chunk, step, lambda copy: copy.start())
        receive(chunk, members - 2)
        for offset in list(range(1, groups)) + [0]:
            peer = lax.rem(group + offset, groups)
            for slot in range(wanted):
                chosen[chunk, offset, slot] = full[chunk][:, ids_ref[peer * wanted + slot]]
            if offset:
                give(chunk, offset).start()
            else:
                mine(chunk).start()
    for chunk in range(chunks):
        for step in range(members - 1):
            forward(chunk, step, lambda copy: copy.wait_send())
        for offset in range(1, groups):
            spread(chunk, offset).wait_send()
            give(chunk, offset).wait_send()
            given(chunk, offset).wait_recv()
        mine(chunk).wait()


def exchange(ids, pieces, groups, members):
    chunks, _, blocks, rows, lanes = pieces.shape
    wanted = ids.shape[0] // groups
    dma = pltpu.SemaphoreType.DMA
    return pl.pallas_call(
        functools.partial(exchange_kernel, groups, members),
        out_shape=jax.ShapeDtypeStruct(
            (chunks, groups, wanted, members, rows, lanes), pieces.dtype
        ),
        in_specs=[
            pl.BlockSpec(memory_space=pltpu.SMEM),
            pl.BlockSpec(memory_space=pl.ANY),
        ],
        out_specs=pl.BlockSpec(memory_space=pl.ANY),
        scratch_shapes=[
            pltpu.VMEM((chunks, groups, wanted, members, rows, lanes), pieces.dtype),
            dma((chunks, groups)),
            dma((chunks, groups)),
            dma((chunks, members)),
            dma((chunks, members)),
            dma((chunks, members)),
            dma((chunks, members)),
            dma((chunks, groups)),
            dma((chunks, groups)),
            dma((2, chunks)),
        ]
        + [
            pltpu.VMEM((members, groups * blocks, rows, lanes), pieces.dtype)
            for _ in range(chunks)
        ],
        compiler_params=pltpu.CompilerParams(
            collective_id=0, has_side_effects=True, vmem_limit_bytes=32 * 2**20
        ),
    )(ids, pieces)


def correlate_kernel(lane_parts, items_ref, lags_ref, out_ref, own, partners, even, odd):
    chunks, pieces, blocks, slabs, rows, chunk_lanes = items_ref.shape
    step = pl.program_id(0)
    pairs = blocks - 1
    depth = own.shape[1]
    block_rows = own.shape[0]
    parts_of_slab = lane_parts * chunks

    def shift(buffer, first):
        cosine, sine = lags_ref[0], lags_ref[1]
        for row in range(TILE):
            line = own[pl.ds(first + row, 1), :]
            for window in range(depth // (2 * BINS)):
                base = window * 2 * BINS
                real = line[:, base : base + BINS]
                imag = line[:, base + BINS : base + 2 * BINS]
                buffer[row * LAGS : (row + 1) * LAGS, base : base + BINS] = (
                    real * cosine + imag * sine
                ).astype(jnp.bfloat16)
                buffer[row * LAGS : (row + 1) * LAGS, base + BINS : base + 2 * BINS] = (
                    imag * cosine - real * sine
                ).astype(jnp.bfloat16)

    def multiply(buffer, first):
        total = jnp.dot(buffer[...], partners[...], preferred_element_type=jnp.float32)
        total = total.astype(jnp.bfloat16)
        for row in range(TILE):
            for pair in range(pairs):
                out_ref[pair, :, (first + row) * block_rows : (first + row + 1) * block_rows] = (
                    total[row * LAGS : (row + 1) * LAGS, pair * block_rows : (pair + 1) * block_rows]
                )

    @pl.when(step == 0)
    def _():
        for slab in range(slabs):
            for place in range(parts_of_slab):
                lane, chunk = place // chunks, place % chunks
                at = (slab * parts_of_slab + place) * chunk_lanes
                parts = range(lane, pieces, lane_parts)
                mine = jnp.concatenate([items_ref[chunk, part, 0, slab] for part in parts], axis=0)
                own[:, at : at + chunk_lanes] = mine.astype(jnp.float32)
                for pair in range(pairs):
                    other = jnp.concatenate(
                        [items_ref[chunk, part, 1 + pair, slab] for part in parts], axis=0
                    )
                    columns = slice(pair * block_rows, (pair + 1) * block_rows)
                    partners[at : at + chunk_lanes, columns] = other.T
        shift(even, 0)

    first = step * 2 * TILE
    shift(odd, first + TILE)
    multiply(even, 0)
    shift(even, lax.rem(first + 2 * TILE, block_rows))
    multiply(odd, TILE)


def correlate(items, block_rows, lane_parts):
    chunks, _, blocks, slabs, _, chunk_lanes = items.shape
    pairs = blocks - 1
    depth = slabs * chunks * chunk_lanes * lane_parts
    windows = depth // (2 * BINS)
    scale = 1.0 / math.sqrt(windows * BINS)
    return pl.pallas_call(
        functools.partial(correlate_kernel, lane_parts),
        grid=(block_rows // (2 * TILE),),
        out_shape=jax.ShapeDtypeStruct((pairs, LAGS, block_rows * block_rows), jnp.bfloat16),
        in_specs=[
            pl.BlockSpec(memory_space=pltpu.VMEM),
            pl.BlockSpec(memory_space=pltpu.VMEM),
        ],
        out_specs=pl.BlockSpec((pairs, LAGS, 2 * TILE * block_rows), lambda i: (0, 0, i)),
        scratch_shapes=[
            pltpu.VMEM((block_rows, depth), jnp.float32),
            pltpu.VMEM((depth, pairs * block_rows), jnp.bfloat16),
            pltpu.VMEM((TILE * LAGS, depth), jnp.bfloat16),
            pltpu.VMEM((TILE * LAGS, depth), jnp.bfloat16),
        ],
        compiler_params=pltpu.CompilerParams(vmem_limit_bytes=48 * 2**20),
        cost_estimate=pl.CostEstimate(
            flops=2 * LAGS * block_rows * depth * pairs * block_rows,
            bytes_accessed=pairs * LAGS * block_rows * block_rows * 2,
            transcendentals=0,
        ),
    )(items, lag_table(scale))


def shards(record, deck_ids, partners):
    groups = lax.axis_size("blk")
    members = lax.axis_size("win")
    group_index = lax.axis_index("blk")
    member_index = lax.axis_index("win")
    block_rows = record.shape[0] // members
    slab_lanes = record.shape[1] // WS * 2 * BINS
    row_parts = block_rows // PIECE_ROWS
    lane_parts = max(1, groups // row_parts)
    lanes = slab_lanes // lane_parts
    rows = block_rows * lane_parts // groups
    chunks = lanes // LANES
    decks = lax.dynamic_slice_in_dim(deck_ids, group_index * members, members, 0)
    pieces = whiten(record, decks, block_rows, (chunks, groups, members, rows, LANES))
    own_ids = jnp.arange(groups, dtype=jnp.int32) * members + member_index
    rows_here = lax.dynamic_index_in_dim(
        partners.reshape(groups, members, -1), member_index, 1, keepdims=False
    )
    ids = jnp.concatenate([own_ids[:, None], rows_here], axis=1)
    items = exchange(ids.reshape(-1), pieces, groups, members)
    return correlate(items, block_rows, lane_parts)


def solution(mesh):
    return jax.shard_map(
        shards,
        mesh=mesh,
        in_specs=(P("blk", "win"), P(), P()),
        out_specs=P(("blk", "win"), None, None),
        check_vma=False,
    )
```

```python
import functools
import math

import jax
import jax.numpy as jnp
import numpy as np
from jax import lax
from jax.experimental import pallas as pl
from jax.experimental.pallas import tpu as pltpu
from jax.sharding import PartitionSpec as P

WS = 512
BINS = 128
LAGS = 64
PIECE_ROWS = 16
LANES = 128
HALF = 64
TILE = 8


def halves(real, imag):
    return np.concatenate([real[:, :HALF], imag[:, :HALF], real[:, HALF:], imag[:, HALF:]], axis=1)


def forward_table():
    phases = np.arange(WS)[:, None] * np.arange(1, BINS + 1)[None, :] % WS
    angles = phases * (2.0 * math.pi / WS)
    return jnp.asarray(halves(np.cos(angles), -np.sin(angles)), jnp.bfloat16)


def lag_table(windows):
    shifts = np.arange(LAGS) - LAGS // 2
    phases = shifts[:, None] * np.arange(1, BINS + 1)[None, :] % WS
    angles = phases * (2.0 * math.pi / WS)
    cosine, sine = np.cos(angles), -np.sin(angles)
    table = np.stack([halves(cosine, cosine), halves(sine, -sine)])
    table = jnp.asarray(table, jnp.bfloat16).astype(jnp.float32)
    return table / math.sqrt(windows * BINS)


class Product:
    def __init__(self, lane_parts, first_chunk, items, lags, own, turned, partners, even, odd):
        self.lane_parts, self.first_chunk, self.items, self.lags = lane_parts, first_chunk, items, lags
        self.own, self.turned, self.partners = own, turned, partners
        self.even, self.odd = even, odd
        chunks, _, _, slabs, _, _ = items.shape
        self.places = [
            (chunk, slab, lane)
            for chunk in range(chunks)
            for slab in range(slabs)
            for lane in range(lane_parts)
        ]

    def load(self):
        block_rows = self.own.shape[0]
        pieces, blocks = self.items.shape[1:3]
        for place, (chunk, slab, lane) in enumerate(self.places):
            here = slice(place * LANES, (place + 1) * LANES)
            parts = range(lane, pieces, self.lane_parts)

            def gathered(slot):
                return jnp.concatenate([self.items[chunk, part, slot, slab] for part in parts], axis=0)

            mine = gathered(0).astype(jnp.float32)
            self.own[:, here] = mine
            self.turned[:, here] = jnp.concatenate([mine[:, HALF:], mine[:, :HALF]], axis=1)
            for pair in range(blocks - 1):
                self.partners[here, pair * block_rows : (pair + 1) * block_rows] = gathered(1 + pair).T

    def shift(self, buffer, first):
        for row in range(TILE):
            line = self.own[pl.ds(first + row, 1), :]
            turned = self.turned[pl.ds(first + row, 1), :]
            for place, (chunk, _, _) in enumerate(self.places):
                here = slice(place * LANES, (place + 1) * LANES)
                half = (self.first_chunk + chunk) % 2
                there = slice(half * LANES, (half + 1) * LANES)
                buffer[row * LAGS : (row + 1) * LAGS, here] = (
                    line[:, here] * self.lags[0, :, there] + turned[:, here] * self.lags[1, :, there]
                ).astype(jnp.bfloat16)

    def unit(self, step, emit):
        first = step * 2 * TILE
        self.shift(self.odd, first + TILE)
        emit(0, self.multiply(self.even))
        self.shift(self.even, lax.rem(first + 2 * TILE, self.own.shape[0]))
        emit(1, self.multiply(self.odd))

    def multiply(self, buffer):
        return jnp.dot(buffer[...], self.partners[...], preferred_element_type=jnp.float32)


def product_scratch(block_rows, depth, pairs):
    return [
        pltpu.VMEM((block_rows, depth), jnp.float32),
        pltpu.VMEM((block_rows, depth), jnp.float32),
        pltpu.VMEM((depth, pairs * block_rows), jnp.bfloat16),
        pltpu.VMEM((TILE * LAGS, depth), jnp.bfloat16),
        pltpu.VMEM((TILE * LAGS, depth), jnp.bfloat16),
    ]


def whiten_kernel(block_rows, deck_ref, record_ref, table_ref, out_ref):
    chunks, pieces, blocks, rows, chunk_lanes = out_ref.shape
    windows = record_ref.shape[1] // WS
    lane_parts = windows * 2 * BINS // (chunks * chunk_lanes)
    for block in range(blocks):
        here = pl.ds(block * block_rows, block_rows)
        polarity = (1 - 2 * deck_ref[block]).astype(jnp.float32)
        values = []
        for window in range(windows):
            spectra = jnp.dot(
                record_ref[here, pl.ds(window * WS, WS)],
                table_ref[...],
                preferred_element_type=jnp.float32,
            )
            power = jnp.sum(spectra * spectra, axis=1, keepdims=True) / BINS
            values.append((spectra * (polarity / jnp.sqrt(power + 1e-06))).astype(jnp.bfloat16))
        whole = jnp.concatenate(values, axis=1)
        for piece in range(pieces):
            row, lane = piece // lane_parts, piece % lane_parts
            for chunk in range(chunks):
                at = (lane * chunks + chunk) * chunk_lanes
                out_ref[chunk, piece, block] = whole[
                    row * rows : (row + 1) * rows, at : at + chunk_lanes
                ]


def whiten(record, decks, block_rows, shape):
    return pl.pallas_call(
        functools.partial(whiten_kernel, block_rows),
        out_shape=jax.ShapeDtypeStruct(shape, jnp.bfloat16),
        in_specs=[
            pl.BlockSpec(memory_space=pltpu.SMEM),
            pl.BlockSpec(memory_space=pltpu.VMEM),
            pl.BlockSpec(memory_space=pltpu.VMEM),
        ],
        out_specs=pl.BlockSpec(memory_space=pltpu.VMEM),
        compiler_params=pltpu.CompilerParams(vmem_limit_bytes=32 * 2**20),
    )(decks, record, forward_table())


def exchange_kernel(
    groups, members, lane_parts, ids_ref, pieces_ref, lags_ref, items_ref, partial_ref, chosen,
    spread_send, spread_recv, up_send, up_recv, down_send, down_recv, give_send, give_recv, local,
    near, stage, stage_sems, own, turned, partners, even, odd, *full
):
    chunks, _, blocks = pieces_ref.shape[:3]
    wanted = items_ref.shape[2]
    early = near.shape[0]
    units = stage.shape[0]
    product = Product(lane_parts, 0, near, lags_ref, own, turned, partners, even, odd)
    group = lax.axis_index("blk")
    member = lax.axis_index("win")
    mesh_id = pl.DeviceIdType.MESH

    barrier = pltpu.get_barrier_semaphore()
    for offset in range(1, groups):
        pl.semaphore_signal(
            barrier, inc=1, device_id=(lax.rem(group + offset, groups), member),
            device_id_type=mesh_id,
        )

    @pl.when(member > 0)
    def _():
        pl.semaphore_signal(
            barrier, inc=1, device_id=(group, member - 1), device_id_type=mesh_id
        )

    @pl.when(member < members - 1)
    def _():
        pl.semaphore_signal(
            barrier, inc=1, device_id=(group, member + 1), device_id_type=mesh_id
        )

    beside = jnp.where(member > 0, 1, 0) + jnp.where(member < members - 1, 1, 0)
    pl.semaphore_wait(barrier, groups - 1 + beside)

    def spread(chunk, offset):
        peer = lax.rem(group + offset, groups)
        return pltpu.make_async_remote_copy(
            src_ref=pieces_ref.at[chunk, peer],
            dst_ref=full[chunk].at[member, pl.ds(group * blocks, blocks)],
            send_sem=spread_send.at[chunk, offset],
            recv_sem=spread_recv.at[chunk, offset],
            device_id=(peer, member),
            device_id_type=mesh_id,
        )

    def arrived(chunk, offset):
        peer = lax.rem(group + groups - offset, groups)
        here = full[chunk].at[member, pl.ds(peer * blocks, blocks)]
        return pltpu.make_async_remote_copy(
            src_ref=here,
            dst_ref=here,
            send_sem=spread_send.at[chunk, offset],
            recv_sem=spread_recv.at[chunk, offset],
            device_id=(peer, member),
            device_id_type=mesh_id,
        )

    def kept(chunk):
        return pltpu.make_async_copy(
            pieces_ref.at[chunk, group],
            full[chunk].at[member, pl.ds(group * blocks, blocks)],
            local.at[0, chunk],
        )

    def up(chunk, step, slab):
        return pltpu.make_async_remote_copy(
            src_ref=full[chunk].at[slab],
            dst_ref=full[chunk].at[slab],
            send_sem=up_send.at[chunk, step],
            recv_sem=up_recv.at[chunk, step],
            device_id=(group, member + 1),
            device_id_type=mesh_id,
        )

    def down(chunk, step, slab):
        return pltpu.make_async_remote_copy(
            src_ref=full[chunk].at[slab],
            dst_ref=full[chunk].at[slab],
            send_sem=down_send.at[chunk, step],
            recv_sem=down_recv.at[chunk, step],
            device_id=(group, member - 1),
            device_id_type=mesh_id,
        )

    def forward(chunk, step, act):
        @pl.when((member < members - 1) & (member >= step))
        def _():
            act(up(chunk, step, member - step))

        @pl.when((member > 0) & (member + step <= members - 1))
        def _():
            act(down(chunk, step, member + step))

    def receive(chunk, step):
        @pl.when(member >= step + 1)
        def _():
            up(chunk, step, member - 1 - step).wait_recv()

        @pl.when(member + 1 + step <= members - 1)
        def _():
            down(chunk, step, member + 1 + step).wait_recv()

    def open_chunk(chunk):
        kept(chunk).wait()
        for offset in range(1, groups):
            arrived(chunk, offset).wait_recv()
        forward(chunk, 0, lambda copy: copy.start())

    def landing(chunk, source):
        return near.at[chunk, source] if chunk < early else items_ref.at[chunk - early, source]

    def give(chunk, offset):
        peer = lax.rem(group + offset, groups)
        return pltpu.make_async_remote_copy(
            src_ref=chosen.at[chunk, offset],
            dst_ref=landing(chunk, group),
            send_sem=give_send.at[chunk, offset],
            recv_sem=give_recv.at[chunk, offset],
            device_id=(peer, member),
            device_id_type=mesh_id,
        )

    def given(chunk, offset):
        peer = lax.rem(group + groups - offset, groups)
        return pltpu.make_async_remote_copy(
            src_ref=chosen.at[chunk, offset],
            dst_ref=landing(chunk, peer),
            send_sem=give_send.at[chunk, offset],
            recv_sem=give_recv.at[chunk, offset],
            device_id=(peer, member),
            device_id_type=mesh_id,
        )

    def mine(chunk):
        return pltpu.make_async_copy(
            chosen.at[chunk, 0], landing(chunk, group), local.at[1, chunk]
        )

    def settle(chunk):
        for offset in range(1, groups):
            given(chunk, offset).wait_recv()
        mine(chunk).wait()

    def stored(step):
        return pltpu.make_async_copy(stage.at[step], partial_ref.at[step], stage_sems.at[step])

    def work(step, carry):
        def emit(side, total):
            stage[step, side * TILE * LAGS : (side + 1) * TILE * LAGS, :] = total

        product.unit(step, emit)
        stored(step).start()
        return carry

    for chunk in range(chunks):
        for offset in range(1, groups):
            spread(chunk, offset).start()
        kept(chunk).start()
    open_chunk(0)
    for chunk in range(chunks):
        if chunk + 1 < chunks:
            open_chunk(chunk + 1)
        for step in range(members - 1):
            if chunk == chunks - 1:
                if step == 0:
                    for before in range(early):
                        settle(before)
                    product.load()
                    product.shift(even, 0)
                work(step, 0)
            receive(chunk, step)
            if step + 1 < members - 1:
                forward(chunk, step + 1, lambda copy: copy.start())
        for offset in list(range(1, groups)) + [0]:
            peer = lax.rem(group + offset, groups)
            for slot in range(wanted):
                chosen[chunk, offset, slot] = full[chunk][:, ids_ref[peer * wanted + slot]]
            if offset:
                give(chunk, offset).start()
            else:
                mine(chunk).start()
    lax.fori_loop(members - 1, units, work, 0)
    for chunk in range(chunks):
        for step in range(members - 1):
            forward(chunk, step, lambda copy: copy.wait_send())
        for offset in range(1, groups):
            spread(chunk, offset).wait_send()
            give(chunk, offset).wait_send()
        if chunk >= early:
            settle(chunk)
    for step in range(units):
        stored(step).wait()


def exchange(ids, pieces, lags, groups, members, block_rows, lane_parts):
    chunks, _, blocks, rows, lanes = pieces.shape
    wanted = ids.shape[0] // groups
    early = chunks // 2
    depth = early * members * lane_parts * lanes
    columns = (wanted - 1) * block_rows
    units = block_rows // (2 * TILE)
    dma = pltpu.SemaphoreType.DMA
    return pl.pallas_call(
        functools.partial(exchange_kernel, groups, members, lane_parts),
        out_shape=(
            jax.ShapeDtypeStruct(
                (chunks - early, groups, wanted, members, rows, lanes), pieces.dtype
            ),
            jax.ShapeDtypeStruct((units, 2 * TILE * LAGS, columns), jnp.float32),
        ),
        in_specs=[
            pl.BlockSpec(memory_space=pltpu.SMEM),
            pl.BlockSpec(memory_space=pl.ANY),
            pl.BlockSpec(memory_space=pltpu.VMEM),
        ],
        out_specs=(pl.BlockSpec(memory_space=pl.ANY), pl.BlockSpec(memory_space=pl.ANY)),
        scratch_shapes=[
            pltpu.VMEM((chunks, groups, wanted, members, rows, lanes), pieces.dtype),
            dma((chunks, groups)),
            dma((chunks, groups)),
            dma((chunks, members)),
            dma((chunks, members)),
            dma((chunks, members)),
            dma((chunks, members)),
            dma((chunks, groups)),
            dma((chunks, groups)),
            dma((2, chunks)),
            pltpu.VMEM((early, groups, wanted, members, rows, lanes), pieces.dtype),
            pltpu.VMEM((units, 2 * TILE * LAGS, columns), jnp.float32),
            dma((units,)),
        ]
        + product_scratch(block_rows, depth, wanted - 1)
        + [
            pltpu.VMEM((members, groups * blocks, rows, lanes), pieces.dtype)
            for _ in range(chunks)
        ],
        compiler_params=pltpu.CompilerParams(
            collective_id=0, has_side_effects=True, vmem_limit_bytes=56 * 2**20
        ),
    )(ids, pieces, lags)


def correlate_kernel(
    lane_parts, early, items_ref, lags_ref, partial_ref, out_ref, own, turned, partners, even, odd
):
    step = pl.program_id(0)
    product = Product(lane_parts, early, items_ref, lags_ref, own, turned, partners, even, odd)
    pairs, block_rows = out_ref.shape[0], own.shape[0]

    @pl.when(step == 0)
    def _():
        product.load()
        product.shift(even, 0)

    def emit(side, total):
        base = side * TILE
        total = total + partial_ref[0, base * LAGS : (base + TILE) * LAGS, :]
        total = total.astype(jnp.bfloat16)
        for row in range(TILE):
            at = (base + row) * block_rows
            for pair in range(pairs):
                out_ref[pair, :, at : at + block_rows] = total[
                    row * LAGS : (row + 1) * LAGS, pair * block_rows : (pair + 1) * block_rows
                ]

    product.unit(step, emit)


def correlate(items, lags, partial, block_rows, lane_parts, early):
    chunks, _, blocks, slabs, _, chunk_lanes = items.shape
    pairs = blocks - 1
    depth = slabs * chunks * chunk_lanes * lane_parts
    return pl.pallas_call(
        functools.partial(correlate_kernel, lane_parts, early),
        grid=(block_rows // (2 * TILE),),
        out_shape=jax.ShapeDtypeStruct((pairs, LAGS, block_rows * block_rows), jnp.bfloat16),
        in_specs=[
            pl.BlockSpec(memory_space=pltpu.VMEM),
            pl.BlockSpec(memory_space=pltpu.VMEM),
            pl.BlockSpec((1,) + partial.shape[1:], lambda i: (i, 0, 0)),
        ],
        out_specs=pl.BlockSpec((pairs, LAGS, 2 * TILE * block_rows), lambda i: (0, 0, i)),
        scratch_shapes=product_scratch(block_rows, depth, pairs),
        compiler_params=pltpu.CompilerParams(vmem_limit_bytes=48 * 2**20),
        cost_estimate=pl.CostEstimate(
            flops=2 * LAGS * block_rows * depth * pairs * block_rows,
            bytes_accessed=pairs * LAGS * block_rows * block_rows * 2,
            transcendentals=0,
        ),
    )(items, lags, partial)


def shards(record, deck_ids, partners):
    groups = lax.axis_size("blk")
    members = lax.axis_size("win")
    group_index = lax.axis_index("blk")
    member_index = lax.axis_index("win")
    block_rows = record.shape[0] // members
    slab_lanes = record.shape[1] // WS * 2 * BINS
    row_parts = block_rows // PIECE_ROWS
    lane_parts = max(1, groups // row_parts)
    lanes = slab_lanes // lane_parts
    rows = block_rows * lane_parts // groups
    chunks = lanes // LANES
    decks = lax.dynamic_slice_in_dim(deck_ids, group_index * members, members, 0)
    pieces = whiten(record, decks, block_rows, (chunks, groups, members, rows, LANES))
    own_ids = jnp.arange(groups, dtype=jnp.int32) * members + member_index
    rows_here = lax.dynamic_index_in_dim(
        partners.reshape(groups, members, -1), member_index, 1, keepdims=False
    )
    ids = jnp.concatenate([own_ids[:, None], rows_here], axis=1)
    lags = lag_table(record.shape[1] // WS * members)
    items, partial = exchange(
        ids.reshape(-1), pieces, lags, groups, members, block_rows, lane_parts
    )
    return correlate(items, lags, partial, block_rows, lane_parts, chunks // 2)


def solution(mesh):
    return jax.shard_map(
        shards,
        mesh=mesh,
        in_specs=(P("blk", "win"), P(), P()),
        out_specs=P(("blk", "win"), None, None),
        check_vma=False,
    )
```

```python
import functools
import math

import jax
import jax.numpy as jnp
import numpy as np
from jax import lax
from jax.experimental import pallas as pl
from jax.experimental.pallas import tpu as pltpu
from jax.sharding import PartitionSpec as P

WS = 512
BINS = 128
LAGS = 64
PIECE_ROWS = 16
LANES = 128
HALF = 64
TILE = 8


def halves(real, imag):
    return np.concatenate([real[:, :HALF], imag[:, :HALF], real[:, HALF:], imag[:, HALF:]], axis=1)


def forward_table():
    phases = np.arange(WS)[:, None] * np.arange(1, BINS + 1)[None, :] % WS
    angles = phases * (2.0 * math.pi / WS)
    return jnp.asarray(halves(np.cos(angles), -np.sin(angles)), jnp.bfloat16)


def lag_table(windows):
    shifts = np.arange(LAGS) - LAGS // 2
    phases = shifts[:, None] * np.arange(1, BINS + 1)[None, :] % WS
    angles = phases * (2.0 * math.pi / WS)
    cosine, sine = np.cos(angles), -np.sin(angles)
    table = np.stack([halves(cosine, cosine), halves(sine, -sine)])
    table = jnp.asarray(table, jnp.bfloat16).astype(jnp.float32)
    return table / math.sqrt(windows * BINS)


class Product:
    def __init__(self, lane_parts, first_chunk, items, lags, own, turned, partners, even, odd):
        self.lane_parts, self.first_chunk, self.items, self.lags = lane_parts, first_chunk, items, lags
        self.own, self.turned, self.partners = own, turned, partners
        self.even, self.odd = even, odd
        chunks, _, _, slabs, _, _ = items.shape
        self.places = [
            (chunk, slab, lane)
            for chunk in range(chunks)
            for slab in range(slabs)
            for lane in range(lane_parts)
        ]

    def load(self):
        block_rows = self.own.shape[0]
        pieces, blocks = self.items.shape[1:3]
        for place, (chunk, slab, lane) in enumerate(self.places):
            here = slice(place * LANES, (place + 1) * LANES)
            parts = range(lane, pieces, self.lane_parts)

            def gathered(slot):
                return jnp.concatenate([self.items[chunk, part, slot, slab] for part in parts], axis=0)

            mine = gathered(0).astype(jnp.float32)
            self.own[:, here] = mine
            self.turned[:, here] = jnp.concatenate([mine[:, HALF:], mine[:, :HALF]], axis=1)
            for pair in range(blocks - 1):
                self.partners[here, pair * block_rows : (pair + 1) * block_rows] = gathered(1 + pair).T

    def shift(self, buffer, first):
        for row in range(TILE):
            line = self.own[pl.ds(first + row, 1), :]
            turned = self.turned[pl.ds(first + row, 1), :]
            for place, (chunk, _, _) in enumerate(self.places):
                here = slice(place * LANES, (place + 1) * LANES)
                half = (self.first_chunk + chunk) % 2
                there = slice(half * LANES, (half + 1) * LANES)
                buffer[row * LAGS : (row + 1) * LAGS, here] = (
                    line[:, here] * self.lags[0, :, there] + turned[:, here] * self.lags[1, :, there]
                ).astype(jnp.bfloat16)

    def unit(self, step, emit):
        first = step * 2 * TILE
        self.shift(self.odd, first + TILE)
        emit(0, self.multiply(self.even))
        self.shift(self.even, lax.rem(first + 2 * TILE, self.own.shape[0]))
        emit(1, self.multiply(self.odd))

    def multiply(self, buffer):
        return jnp.dot(buffer[...], self.partners[...], preferred_element_type=jnp.float32)


def product_scratch(block_rows, depth, pairs):
    return [
        pltpu.VMEM((block_rows, depth), jnp.float32),
        pltpu.VMEM((block_rows, depth), jnp.float32),
        pltpu.VMEM((depth, pairs * block_rows), jnp.bfloat16),
        pltpu.VMEM((TILE * LAGS, depth), jnp.bfloat16),
        pltpu.VMEM((TILE * LAGS, depth), jnp.bfloat16),
    ]


def whiten_kernel(block_rows, deck_ref, record_ref, table_ref, out_ref):
    chunks, pieces, blocks, rows, chunk_lanes = out_ref.shape
    first_block = lax.axis_index("blk") * blocks
    windows = record_ref.shape[1] // WS
    lane_parts = windows * 2 * BINS // (chunks * chunk_lanes)
    for block in range(blocks):
        here = pl.ds(block * block_rows, block_rows)
        polarity = (1 - 2 * deck_ref[first_block + block]).astype(jnp.float32)
        values = []
        for window in range(windows):
            spectra = jnp.dot(
                record_ref[here, pl.ds(window * WS, WS)],
                table_ref[...],
                preferred_element_type=jnp.float32,
            )
            power = jnp.sum(spectra * spectra, axis=1, keepdims=True) / BINS
            values.append((spectra * (polarity / jnp.sqrt(power + 1e-06))).astype(jnp.bfloat16))
        whole = jnp.concatenate(values, axis=1)
        for piece in range(pieces):
            row, lane = piece // lane_parts, piece % lane_parts
            for chunk in range(chunks):
                at = (lane * chunks + chunk) * chunk_lanes
                out_ref[chunk, piece, block] = whole[
                    row * rows : (row + 1) * rows, at : at + chunk_lanes
                ]


def whiten(record, decks, block_rows, shape):
    return pl.pallas_call(
        functools.partial(whiten_kernel, block_rows),
        out_shape=jax.ShapeDtypeStruct(shape, jnp.bfloat16),
        in_specs=[
            pl.BlockSpec(memory_space=pltpu.SMEM),
            pl.BlockSpec(memory_space=pltpu.VMEM),
            pl.BlockSpec(memory_space=pltpu.VMEM),
        ],
        out_specs=pl.BlockSpec(memory_space=pltpu.VMEM),
        compiler_params=pltpu.CompilerParams(vmem_limit_bytes=32 * 2**20),
    )(decks, record, forward_table())


def exchange_kernel(
    groups, members, lane_parts, partners_ref, pieces_ref, lags_ref, items_ref, partial_ref, chosen,
    spread_send, spread_recv, up_send, up_recv, down_send, down_recv, give_send, give_recv, local,
    near, stage, stage_sems, own, turned, partners, even, odd, *full
):
    chunks, _, blocks = pieces_ref.shape[:3]
    wanted = items_ref.shape[2]
    early = near.shape[0]
    units = stage.shape[0]
    product = Product(lane_parts, 0, near, lags_ref, own, turned, partners, even, odd)
    group = lax.axis_index("blk")
    member = lax.axis_index("win")
    mesh_id = pl.DeviceIdType.MESH

    barrier = pltpu.get_barrier_semaphore()
    for offset in range(1, groups):
        pl.semaphore_signal(
            barrier, inc=1, device_id=(lax.rem(group + offset, groups), member),
            device_id_type=mesh_id,
        )

    @pl.when(member > 0)
    def _():
        pl.semaphore_signal(
            barrier, inc=1, device_id=(group, member - 1), device_id_type=mesh_id
        )

    @pl.when(member < members - 1)
    def _():
        pl.semaphore_signal(
            barrier, inc=1, device_id=(group, member + 1), device_id_type=mesh_id
        )

    beside = jnp.where(member > 0, 1, 0) + jnp.where(member < members - 1, 1, 0)
    pl.semaphore_wait(barrier, groups - 1 + beside)

    def spread(chunk, offset):
        peer = lax.rem(group + offset, groups)
        return pltpu.make_async_remote_copy(
            src_ref=pieces_ref.at[chunk, peer],
            dst_ref=full[chunk].at[member, pl.ds(group * blocks, blocks)],
            send_sem=spread_send.at[chunk, offset],
            recv_sem=spread_recv.at[chunk, offset],
            device_id=(peer, member),
            device_id_type=mesh_id,
        )

    def arrived(chunk, offset):
        peer = lax.rem(group + groups - offset, groups)
        here = full[chunk].at[member, pl.ds(peer * blocks, blocks)]
        return pltpu.make_async_remote_copy(
            src_ref=here,
            dst_ref=here,
            send_sem=spread_send.at[chunk, offset],
            recv_sem=spread_recv.at[chunk, offset],
            device_id=(peer, member),
            device_id_type=mesh_id,
        )

    def kept(chunk):
        return pltpu.make_async_copy(
            pieces_ref.at[chunk, group],
            full[chunk].at[member, pl.ds(group * blocks, blocks)],
            local.at[0, chunk],
        )

    def up(chunk, step, slab):
        return pltpu.make_async_remote_copy(
            src_ref=full[chunk].at[slab],
            dst_ref=full[chunk].at[slab],
            send_sem=up_send.at[chunk, step],
            recv_sem=up_recv.at[chunk, step],
            device_id=(group, member + 1),
            device_id_type=mesh_id,
        )

    def down(chunk, step, slab):
        return pltpu.make_async_remote_copy(
            src_ref=full[chunk].at[slab],
            dst_ref=full[chunk].at[slab],
            send_sem=down_send.at[chunk, step],
            recv_sem=down_recv.at[chunk, step],
            device_id=(group, member - 1),
            device_id_type=mesh_id,
        )

    def forward(chunk, step, act):
        @pl.when((member < members - 1) & (member >= step))
        def _():
            act(up(chunk, step, member - step))

        @pl.when((member > 0) & (member + step <= members - 1))
        def _():
            act(down(chunk, step, member + step))

    def receive(chunk, step):
        @pl.when(member >= step + 1)
        def _():
            up(chunk, step, member - 1 - step).wait_recv()

        @pl.when(member + 1 + step <= members - 1)
        def _():
            down(chunk, step, member + 1 + step).wait_recv()

    def open_chunk(chunk):
        kept(chunk).wait()
        for offset in range(1, groups):
            arrived(chunk, offset).wait_recv()
        forward(chunk, 0, lambda copy: copy.start())

    def landing(chunk, source):
        return near.at[chunk, source] if chunk < early else items_ref.at[chunk - early, source]

    def give(chunk, offset):
        peer = lax.rem(group + offset, groups)
        return pltpu.make_async_remote_copy(
            src_ref=chosen.at[chunk, offset],
            dst_ref=landing(chunk, group),
            send_sem=give_send.at[chunk, offset],
            recv_sem=give_recv.at[chunk, offset],
            device_id=(peer, member),
            device_id_type=mesh_id,
        )

    def given(chunk, offset):
        peer = lax.rem(group + groups - offset, groups)
        return pltpu.make_async_remote_copy(
            src_ref=chosen.at[chunk, offset],
            dst_ref=landing(chunk, peer),
            send_sem=give_send.at[chunk, offset],
            recv_sem=give_recv.at[chunk, offset],
            device_id=(peer, member),
            device_id_type=mesh_id,
        )

    def mine(chunk):
        return pltpu.make_async_copy(
            chosen.at[chunk, 0], landing(chunk, group), local.at[1, chunk]
        )

    def settle(chunk):
        for offset in range(1, groups):
            given(chunk, offset).wait_recv()
        mine(chunk).wait()

    def stored(step):
        return pltpu.make_async_copy(stage.at[step], partial_ref.at[step], stage_sems.at[step])

    def work(step, carry):
        def emit(side, total):
            stage[step, side * TILE * LAGS : (side + 1) * TILE * LAGS, :] = total

        product.unit(step, emit)
        stored(step).start()
        return carry

    for chunk in range(chunks):
        for offset in range(1, groups):
            spread(chunk, offset).start()
        kept(chunk).start()
    open_chunk(0)
    for chunk in range(chunks):
        if chunk + 1 < chunks:
            open_chunk(chunk + 1)
        for step in range(members - 1):
            if chunk == chunks - 1:
                if step == 0:
                    for before in range(early):
                        settle(before)
                    product.load()
                    product.shift(even, 0)
                work(step, 0)
            receive(chunk, step)
            if step + 1 < members - 1:
                forward(chunk, step + 1, lambda copy: copy.start())
        for offset in list(range(1, groups)) + [0]:
            peer = lax.rem(group + offset, groups)
            for slot in range(wanted):
                item = peer * members + member
                if slot:
                    item = partners_ref[item, slot - 1]
                chosen[chunk, offset, slot] = full[chunk][:, item]
            if offset:
                give(chunk, offset).start()
            else:
                mine(chunk).start()
    lax.fori_loop(members - 1, units, work, 0)
    for chunk in range(chunks):
        for step in range(members - 1):
            forward(chunk, step, lambda copy: copy.wait_send())
        for offset in range(1, groups):
            spread(chunk, offset).wait_send()
            give(chunk, offset).wait_send()
        if chunk >= early:
            settle(chunk)
    for step in range(units):
        stored(step).wait()


def exchange(listed, pieces, lags, groups, members, block_rows, lane_parts):
    chunks, _, blocks, rows, lanes = pieces.shape
    wanted = 1 + listed.shape[1]
    early = chunks // 2
    depth = early * members * lane_parts * lanes
    columns = (wanted - 1) * block_rows
    units = block_rows // (2 * TILE)
    dma = pltpu.SemaphoreType.DMA
    return pl.pallas_call(
        functools.partial(exchange_kernel, groups, members, lane_parts),
        out_shape=(
            jax.ShapeDtypeStruct(
                (chunks - early, groups, wanted, members, rows, lanes), pieces.dtype
            ),
            jax.ShapeDtypeStruct((units, 2 * TILE * LAGS, columns), jnp.float32),
        ),
        in_specs=[
            pl.BlockSpec(memory_space=pltpu.SMEM),
            pl.BlockSpec(memory_space=pl.ANY),
            pl.BlockSpec(memory_space=pltpu.VMEM),
        ],
        out_specs=(pl.BlockSpec(memory_space=pl.ANY), pl.BlockSpec(memory_space=pl.ANY)),
        scratch_shapes=[
            pltpu.VMEM((chunks, groups, wanted, members, rows, lanes), pieces.dtype),
            dma((chunks, groups)),
            dma((chunks, groups)),
            dma((chunks, members)),
            dma((chunks, members)),
            dma((chunks, members)),
            dma((chunks, members)),
            dma((chunks, groups)),
            dma((chunks, groups)),
            dma((2, chunks)),
            pltpu.VMEM((early, groups, wanted, members, rows, lanes), pieces.dtype),
            pltpu.VMEM((units, 2 * TILE * LAGS, columns), jnp.float32),
            dma((units,)),
        ]
        + product_scratch(block_rows, depth, wanted - 1)
        + [
            pltpu.VMEM((members, groups * blocks, rows, lanes), pieces.dtype)
            for _ in range(chunks)
        ],
        compiler_params=pltpu.CompilerParams(
            collective_id=0, has_side_effects=True, vmem_limit_bytes=56 * 2**20
        ),
    )(listed, pieces, lags)


def correlate_kernel(
    lane_parts, early, items_ref, lags_ref, partial_ref, out_ref, own, turned, partners, even, odd
):
    step = pl.program_id(0)
    product = Product(lane_parts, early, items_ref, lags_ref, own, turned, partners, even, odd)
    pairs, block_rows = out_ref.shape[0], own.shape[0]

    @pl.when(step == 0)
    def _():
        product.load()
        product.shift(even, 0)

    def emit(side, total):
        base = side * TILE
        total = total + partial_ref[0, base * LAGS : (base + TILE) * LAGS, :]
        total = total.astype(jnp.bfloat16)
        for row in range(TILE):
            at = (base + row) * block_rows
            for pair in range(pairs):
                out_ref[pair, :, at : at + block_rows] = total[
                    row * LAGS : (row + 1) * LAGS, pair * block_rows : (pair + 1) * block_rows
                ]

    product.unit(step, emit)


def correlate(items, lags, partial, block_rows, lane_parts, early):
    chunks, _, blocks, slabs, _, chunk_lanes = items.shape
    pairs = blocks - 1
    depth = slabs * chunks * chunk_lanes * lane_parts
    return pl.pallas_call(
        functools.partial(correlate_kernel, lane_parts, early),
        grid=(block_rows // (2 * TILE),),
        out_shape=jax.ShapeDtypeStruct((pairs, LAGS, block_rows * block_rows), jnp.bfloat16),
        in_specs=[
            pl.BlockSpec(memory_space=pltpu.VMEM),
            pl.BlockSpec(memory_space=pltpu.VMEM),
            pl.BlockSpec((1,) + partial.shape[1:], lambda i: (i, 0, 0)),
        ],
        out_specs=pl.BlockSpec((pairs, LAGS, 2 * TILE * block_rows), lambda i: (0, 0, i)),
        scratch_shapes=product_scratch(block_rows, depth, pairs),
        compiler_params=pltpu.CompilerParams(vmem_limit_bytes=48 * 2**20),
        cost_estimate=pl.CostEstimate(
            flops=2 * LAGS * block_rows * depth * pairs * block_rows,
            bytes_accessed=pairs * LAGS * block_rows * block_rows * 2,
            transcendentals=0,
        ),
    )(items, lags, partial)


def shards(record, deck_ids, partners):
    groups = lax.axis_size("blk")
    members = lax.axis_size("win")
    block_rows = record.shape[0] // members
    slab_lanes = record.shape[1] // WS * 2 * BINS
    row_parts = block_rows // PIECE_ROWS
    lane_parts = max(1, groups // row_parts)
    lanes = slab_lanes // lane_parts
    rows = block_rows * lane_parts // groups
    chunks = lanes // LANES
    pieces = whiten(record, deck_ids, block_rows, (chunks, groups, members, rows, LANES))
    lags = lag_table(record.shape[1] // WS * members)
    items, partial = exchange(
        partners, pieces, lags, groups, members, block_rows, lane_parts
    )
    return correlate(items, lags, partial, block_rows, lane_parts, chunks // 2)


def solution(mesh):
    return jax.shard_map(
        shards,
        mesh=mesh,
        in_specs=(P("blk", "win"), P(), P()),
        out_specs=P(("blk", "win"), None, None),
        check_vma=False,
    )
```

```python
import functools
import math

import jax
import jax.numpy as jnp
import numpy as np
from jax import lax
from jax.experimental import pallas as pl
from jax.experimental.pallas import tpu as pltpu
from jax.sharding import PartitionSpec as P

WS = 512
BINS = 128
LAGS = 64
PIECE_ROWS = 16
LANES = 128
HALF = 64
TILE = 8


def halves(real, imag):
    return np.concatenate([real[:, :HALF], imag[:, :HALF], real[:, HALF:], imag[:, HALF:]], axis=1)


def forward_table():
    phases = np.arange(WS)[:, None] * np.arange(1, BINS + 1)[None, :] % WS
    angles = phases * (2.0 * math.pi / WS)
    return jnp.asarray(halves(np.cos(angles), -np.sin(angles)), jnp.bfloat16)


def lag_table(windows):
    shifts = np.arange(LAGS) - LAGS // 2
    phases = shifts[:, None] * np.arange(1, BINS + 1)[None, :] % WS
    angles = phases * (2.0 * math.pi / WS)
    cosine, sine = np.cos(angles), -np.sin(angles)
    table = np.stack([halves(cosine, cosine), halves(sine, -sine)])
    table = jnp.asarray(table, jnp.bfloat16).astype(jnp.float32)
    return table / math.sqrt(windows * BINS)


class Product:
    def __init__(self, lane_parts, first_chunk, items, lags, own, turned, partners, even, odd):
        self.lane_parts, self.first_chunk, self.items, self.lags = lane_parts, first_chunk, items, lags
        self.own, self.turned, self.partners = own, turned, partners
        self.even, self.odd = even, odd
        chunks, _, _, slabs, _, _ = items.shape
        self.places = [
            (chunk, slab, lane)
            for chunk in range(chunks)
            for slab in range(slabs)
            for lane in range(lane_parts)
        ]

    def load(self):
        block_rows = self.own.shape[0]
        pieces, blocks = self.items.shape[1:3]
        for place, (chunk, slab, lane) in enumerate(self.places):
            here = slice(place * LANES, (place + 1) * LANES)
            parts = range(lane, pieces, self.lane_parts)

            def gathered(slot):
                return jnp.concatenate([self.items[chunk, part, slot, slab] for part in parts], axis=0)

            mine = gathered(0).astype(jnp.float32)
            self.own[:, here] = mine
            self.turned[:, here] = jnp.concatenate([mine[:, HALF:], mine[:, :HALF]], axis=1)
            for pair in range(blocks - 1):
                self.partners[here, pair * block_rows : (pair + 1) * block_rows] = gathered(1 + pair).T

    def shift(self, buffer, first):
        for row in range(TILE):
            line = self.own[pl.ds(first + row, 1), :]
            turned = self.turned[pl.ds(first + row, 1), :]
            for place, (chunk, _, _) in enumerate(self.places):
                here = slice(place * LANES, (place + 1) * LANES)
                half = (self.first_chunk + chunk) % 2
                there = slice(half * LANES, (half + 1) * LANES)
                buffer[row * LAGS : (row + 1) * LAGS, here] = (
                    line[:, here] * self.lags[0, :, there] + turned[:, here] * self.lags[1, :, there]
                ).astype(jnp.bfloat16)

    def unit(self, step, emit):
        first = step * 2 * TILE
        self.shift(self.odd, first + TILE)
        emit(0, self.multiply(self.even))
        self.shift(self.even, lax.rem(first + 2 * TILE, self.own.shape[0]))
        emit(1, self.multiply(self.odd))

    def multiply(self, buffer):
        return jnp.dot(buffer[...], self.partners[...], preferred_element_type=jnp.float32)


def product_scratch(block_rows, depth, pairs):
    return [
        pltpu.VMEM((block_rows, depth), jnp.float32),
        pltpu.VMEM((block_rows, depth), jnp.float32),
        pltpu.VMEM((depth, pairs * block_rows), jnp.bfloat16),
        pltpu.VMEM((TILE * LAGS, depth), jnp.bfloat16),
        pltpu.VMEM((TILE * LAGS, depth), jnp.bfloat16),
    ]


def whiten_kernel(block_rows, deck_ref, record_ref, table_ref, out_ref):
    chunks, pieces, blocks, rows, chunk_lanes = out_ref.shape
    first_block = lax.axis_index("blk") * blocks
    windows = record_ref.shape[1] // WS
    lane_parts = windows * 2 * BINS // (chunks * chunk_lanes)
    for block in range(blocks):
        here = pl.ds(block * block_rows, block_rows)
        polarity = (1 - 2 * deck_ref[first_block + block]).astype(jnp.float32)
        values = []
        for window in range(windows):
            spectra = jnp.dot(
                record_ref[here, pl.ds(window * WS, WS)],
                table_ref[...],
                preferred_element_type=jnp.float32,
            )
            power = jnp.sum(spectra * spectra, axis=1, keepdims=True) / BINS
            values.append((spectra * (polarity / jnp.sqrt(power + 1e-06))).astype(jnp.bfloat16))
        whole = jnp.concatenate(values, axis=1)
        for piece in range(pieces):
            row, lane = piece // lane_parts, piece % lane_parts
            for chunk in range(chunks):
                at = (lane * chunks + chunk) * chunk_lanes
                out_ref[chunk, piece, block] = whole[
                    row * rows : (row + 1) * rows, at : at + chunk_lanes
                ]


def whiten(record, decks, block_rows, shape):
    return pl.pallas_call(
        functools.partial(whiten_kernel, block_rows),
        out_shape=jax.ShapeDtypeStruct(shape, jnp.bfloat16),
        in_specs=[
            pl.BlockSpec(memory_space=pltpu.SMEM),
            pl.BlockSpec(memory_space=pltpu.VMEM),
            pl.BlockSpec(memory_space=pltpu.VMEM),
        ],
        out_specs=pl.BlockSpec(memory_space=pltpu.VMEM),
        compiler_params=pltpu.CompilerParams(vmem_limit_bytes=32 * 2**20),
    )(decks, record, forward_table())


def exchange_kernel(
    groups, members, lane_parts, partners_ref, pieces_ref, lags_ref, items_ref, partial_ref, chosen,
    spread_send, spread_recv, up_send, up_recv, down_send, down_recv, give_send, give_recv, local,
    near, stage, stage_sems, own, turned, partners, even, odd, *full
):
    chunks, _, blocks = pieces_ref.shape[:3]
    wanted = items_ref.shape[2]
    early = near.shape[0]
    units = stage.shape[0]
    product = Product(lane_parts, 0, near, lags_ref, own, turned, partners, even, odd)
    group = lax.axis_index("blk")
    member = lax.axis_index("win")
    mesh_id = pl.DeviceIdType.MESH

    barrier = pltpu.get_barrier_semaphore()
    for offset in range(1, groups):
        pl.semaphore_signal(
            barrier, inc=1, device_id=(lax.rem(group + offset, groups), member),
            device_id_type=mesh_id,
        )

    @pl.when(member > 0)
    def _():
        pl.semaphore_signal(
            barrier, inc=1, device_id=(group, member - 1), device_id_type=mesh_id
        )

    @pl.when(member < members - 1)
    def _():
        pl.semaphore_signal(
            barrier, inc=1, device_id=(group, member + 1), device_id_type=mesh_id
        )

    beside = jnp.where(member > 0, 1, 0) + jnp.where(member < members - 1, 1, 0)
    pl.semaphore_wait(barrier, groups - 1 + beside)

    def spread(chunk, offset):
        peer = lax.rem(group + offset, groups)
        return pltpu.make_async_remote_copy(
            src_ref=pieces_ref.at[chunk, peer],
            dst_ref=full[chunk].at[member, pl.ds(group * blocks, blocks)],
            send_sem=spread_send.at[chunk, offset],
            recv_sem=spread_recv.at[chunk, offset],
            device_id=(peer, member),
            device_id_type=mesh_id,
        )

    def arrived(chunk, offset):
        peer = lax.rem(group + groups - offset, groups)
        here = full[chunk].at[member, pl.ds(peer * blocks, blocks)]
        return pltpu.make_async_remote_copy(
            src_ref=here,
            dst_ref=here,
            send_sem=spread_send.at[chunk, offset],
            recv_sem=spread_recv.at[chunk, offset],
            device_id=(peer, member),
            device_id_type=mesh_id,
        )

    def kept(chunk):
        return pltpu.make_async_copy(
            pieces_ref.at[chunk, group],
            full[chunk].at[member, pl.ds(group * blocks, blocks)],
            local.at[0, chunk],
        )

    def up(chunk, step, slab):
        return pltpu.make_async_remote_copy(
            src_ref=full[chunk].at[slab],
            dst_ref=full[chunk].at[slab],
            send_sem=up_send.at[chunk, step],
            recv_sem=up_recv.at[chunk, step],
            device_id=(group, member + 1),
            device_id_type=mesh_id,
        )

    def down(chunk, step, slab):
        return pltpu.make_async_remote_copy(
            src_ref=full[chunk].at[slab],
            dst_ref=full[chunk].at[slab],
            send_sem=down_send.at[chunk, step],
            recv_sem=down_recv.at[chunk, step],
            device_id=(group, member - 1),
            device_id_type=mesh_id,
        )

    def forward(chunk, step, act):
        @pl.when((member < members - 1) & (member >= step))
        def _():
            act(up(chunk, step, member - step))

        @pl.when((member > 0) & (member + step <= members - 1))
        def _():
            act(down(chunk, step, member + step))

    def receive(chunk, step):
        @pl.when(member >= step + 1)
        def _():
            up(chunk, step, member - 1 - step).wait_recv()

        @pl.when(member + 1 + step <= members - 1)
        def _():
            down(chunk, step, member + 1 + step).wait_recv()

    def open_chunk(chunk):
        kept(chunk).wait()
        for offset in range(1, groups):
            arrived(chunk, offset).wait_recv()
        forward(chunk, 0, lambda copy: copy.start())

    def landing(chunk, source):
        return near.at[chunk, source] if chunk < early else items_ref.at[chunk - early, source]

    def give(chunk, offset):
        peer = lax.rem(group + offset, groups)
        return pltpu.make_async_remote_copy(
            src_ref=chosen.at[chunk, offset],
            dst_ref=landing(chunk, group),
            send_sem=give_send.at[chunk, offset],
            recv_sem=give_recv.at[chunk, offset],
            device_id=(peer, member),
            device_id_type=mesh_id,
        )

    def given(chunk, offset):
        peer = lax.rem(group + groups - offset, groups)
        return pltpu.make_async_remote_copy(
            src_ref=chosen.at[chunk, offset],
            dst_ref=landing(chunk, peer),
            send_sem=give_send.at[chunk, offset],
            recv_sem=give_recv.at[chunk, offset],
            device_id=(peer, member),
            device_id_type=mesh_id,
        )

    def mine(chunk):
        return pltpu.make_async_copy(
            chosen.at[chunk, 0], landing(chunk, group), local.at[1, chunk]
        )

    def settle(chunk):
        for offset in range(1, groups):
            given(chunk, offset).wait_recv()
        mine(chunk).wait()

    def stored(step):
        return pltpu.make_async_copy(stage.at[step], partial_ref.at[step], stage_sems.at[step])

    def work(step, carry):
        def emit(side, total):
            stage[step, side * TILE * LAGS : (side + 1) * TILE * LAGS, :] = total

        product.unit(step, emit)
        stored(step).start()
        return carry

    for chunk in range(chunks):
        for offset in range(1, groups):
            spread(chunk, offset).start()
        kept(chunk).start()
    open_chunk(0)
    for chunk in range(chunks):
        if chunk + 1 < chunks:
            open_chunk(chunk + 1)
        for step in range(members - 1):
            receive(chunk, step)
            if step + 1 < members - 1:
                forward(chunk, step + 1, lambda copy: copy.start())
            if chunk == chunks - 1 and step == 0:
                for before in range(early):
                    settle(before)
                product.load()
                product.shift(even, 0)
            elif chunk == chunks - 1 and step + 1 < members - 1:
                work(step - 1, 0)
        for offset in list(range(1, groups)) + [0]:
            peer = lax.rem(group + offset, groups)
            for slot in range(wanted):
                item = peer * members + member
                if slot:
                    item = partners_ref[item, slot - 1]
                chosen[chunk, offset, slot] = full[chunk][:, item]
            if offset:
                give(chunk, offset).start()
            else:
                mine(chunk).start()
    lax.fori_loop(members - 3, units, work, 0)
    for chunk in range(chunks):
        for step in range(members - 1):
            forward(chunk, step, lambda copy: copy.wait_send())
        for offset in range(1, groups):
            spread(chunk, offset).wait_send()
            give(chunk, offset).wait_send()
        if chunk >= early:
            settle(chunk)
    for step in range(units):
        stored(step).wait()


def exchange(listed, pieces, lags, groups, members, block_rows, lane_parts):
    chunks, _, blocks, rows, lanes = pieces.shape
    wanted = 1 + listed.shape[1]
    early = chunks // 2
    depth = early * members * lane_parts * lanes
    columns = (wanted - 1) * block_rows
    units = block_rows // (2 * TILE)
    dma = pltpu.SemaphoreType.DMA
    return pl.pallas_call(
        functools.partial(exchange_kernel, groups, members, lane_parts),
        out_shape=(
            jax.ShapeDtypeStruct(
                (chunks - early, groups, wanted, members, rows, lanes), pieces.dtype
            ),
            jax.ShapeDtypeStruct((units, 2 * TILE * LAGS, columns), jnp.float32),
        ),
        in_specs=[
            pl.BlockSpec(memory_space=pltpu.SMEM),
            pl.BlockSpec(memory_space=pl.ANY),
            pl.BlockSpec(memory_space=pltpu.VMEM),
        ],
        out_specs=(pl.BlockSpec(memory_space=pl.ANY), pl.BlockSpec(memory_space=pl.ANY)),
        scratch_shapes=[
            pltpu.VMEM((chunks, groups, wanted, members, rows, lanes), pieces.dtype),
            dma((chunks, groups)),
            dma((chunks, groups)),
            dma((chunks, members)),
            dma((chunks, members)),
            dma((chunks, members)),
            dma((chunks, members)),
            dma((chunks, groups)),
            dma((chunks, groups)),
            dma((2, chunks)),
            pltpu.VMEM((early, groups, wanted, members, rows, lanes), pieces.dtype),
            pltpu.VMEM((units, 2 * TILE * LAGS, columns), jnp.float32),
            dma((units,)),
        ]
        + product_scratch(block_rows, depth, wanted - 1)
        + [
            pltpu.VMEM((members, groups * blocks, rows, lanes), pieces.dtype)
            for _ in range(chunks)
        ],
        compiler_params=pltpu.CompilerParams(
            collective_id=0, has_side_effects=True, vmem_limit_bytes=56 * 2**20
        ),
    )(listed, pieces, lags)


def correlate_kernel(
    lane_parts, early, items_ref, lags_ref, partial_ref, out_ref, own, turned, partners, even, odd
):
    step = pl.program_id(0)
    product = Product(lane_parts, early, items_ref, lags_ref, own, turned, partners, even, odd)
    pairs, block_rows = out_ref.shape[0], own.shape[0]

    @pl.when(step == 0)
    def _():
        product.load()
        product.shift(even, 0)

    def emit(side, total):
        base = side * TILE
        total = total + partial_ref[0, base * LAGS : (base + TILE) * LAGS, :]
        total = total.astype(jnp.bfloat16)
        for row in range(TILE):
            at = (base + row) * block_rows
            for pair in range(pairs):
                out_ref[pair, :, at : at + block_rows] = total[
                    row * LAGS : (row + 1) * LAGS, pair * block_rows : (pair + 1) * block_rows
                ]

    product.unit(step, emit)


def correlate(items, lags, partial, block_rows, lane_parts, early):
    chunks, _, blocks, slabs, _, chunk_lanes = items.shape
    pairs = blocks - 1
    depth = slabs * chunks * chunk_lanes * lane_parts
    return pl.pallas_call(
        functools.partial(correlate_kernel, lane_parts, early),
        grid=(block_rows // (2 * TILE),),
        out_shape=jax.ShapeDtypeStruct((pairs, LAGS, block_rows * block_rows), jnp.bfloat16),
        in_specs=[
            pl.BlockSpec(memory_space=pltpu.VMEM),
            pl.BlockSpec(memory_space=pltpu.VMEM),
            pl.BlockSpec((1,) + partial.shape[1:], lambda i: (i, 0, 0)),
        ],
        out_specs=pl.BlockSpec((pairs, LAGS, 2 * TILE * block_rows), lambda i: (0, 0, i)),
        scratch_shapes=product_scratch(block_rows, depth, pairs),
        compiler_params=pltpu.CompilerParams(vmem_limit_bytes=48 * 2**20),
        cost_estimate=pl.CostEstimate(
            flops=2 * LAGS * block_rows * depth * pairs * block_rows,
            bytes_accessed=pairs * LAGS * block_rows * block_rows * 2,
            transcendentals=0,
        ),
    )(items, lags, partial)


def shards(record, deck_ids, partners):
    groups = lax.axis_size("blk")
    members = lax.axis_size("win")
    block_rows = record.shape[0] // members
    slab_lanes = record.shape[1] // WS * 2 * BINS
    row_parts = block_rows // PIECE_ROWS
    lane_parts = max(1, groups // row_parts)
    lanes = slab_lanes // lane_parts
    rows = block_rows * lane_parts // groups
    chunks = lanes // LANES
    pieces = whiten(record, deck_ids, block_rows, (chunks, groups, members, rows, LANES))
    lags = lag_table(record.shape[1] // WS * members)
    items, partial = exchange(
        partners, pieces, lags, groups, members, block_rows, lane_parts
    )
    return correlate(items, lags, partial, block_rows, lane_parts, chunks // 2)


def solution(mesh):
    return jax.shard_map(
        shards,
        mesh=mesh,
        in_specs=(P("blk", "win"), P(), P()),
        out_specs=P(("blk", "win"), None, None),
        check_vma=False,
    )
```
